128 devices in a mesh: blk: 32 (over y_lo, z, x), rep: 4 (over y_hi, core).
Axes of the slice: x: 4, y: 4 (y_hi: 2, y_lo: 2; y = y_hi * 2 + y_lo), z: 4, core: 2. Of those that a mesh axis runs over, the one named last changes fastest.
Arguments:
- features: bfloat16 [65536, 256], P(('blk', 'rep')), may hold values from -6 to 6
- tiles: bfloat16 [32, 4, 32, 12, 128, 128], P('blk', 'rep'), may hold values from -0.1875 to 0.1875
- patch_horizontal_bands: int32 [32, 4, 32, 12], P('blk', 'rep'), may hold values from 0 to 15, as said below
- patch_vertical_bands: int32 [32, 4, 32, 12], P('blk', 'rep'), may hold values from 0 to 3
- active_patch_numbers: int32 [32, 4, 32], P('blk', 'rep'), may hold values from 1 to 12, as said below
- weight: bfloat16 [256, 256], replicated, may hold values from -0.375 to 0.375
- cotangent: bfloat16 [65536, 256], P(('blk', 'rep')), may hold values from -6 to 6
Outputs:
- output: bfloat16 [65536, 256], P(('blk', 'rep'))
- grad_weight: float32 [256, 256], replicated
- grad_input: float32 [65536, 256], P(('blk', 'rep'))
The draws below stay inside these ranges and needn't reach their ends.
Inputs may be any that keep to these rules, and one draw needn't show every extreme that they name: Within the first active_patch_numbers entries of a list, the pairs (patch_horizontal_bands, patch_vertical_bands) are distinct. active_patch_numbers[g, r, g] is 12 for every g and r.
All inputs are finite; a program needn't handle non-finite values.
Results may differ from the reference program's by a relative error of at most 0.0057.
Values may be sent and summed in bfloat16 or wider, within the bound.
A program may use at most 64 MiB of HBM per device.

```python
import math
import jax
import jax.numpy as jnp
from jax import lax

F = 256
BS = 128
BANDS_ON_CHIPSET = 4
CAP = 12
BANDS_IN_STRIPE = 16
ROWS = 65536
N_BLK = 32
N_REP = 4


def tile_layout(key):
    positions = BANDS_ON_CHIPSET * BANDS_ON_CHIPSET * N_REP
    scores = jax.random.randint(jax.random.fold_in(key, 11), (N_BLK, N_REP, N_BLK, positions), 0, 2 ** 20)
    scores = scores * positions + jnp.arange(positions, dtype=jnp.int32)
    return jnp.argsort(scores, axis=-1)[..., :CAP].astype(jnp.int32)


def draw_patch_horizontal_bands(key, part):
    return (tile_layout(key) // BANDS_ON_CHIPSET).astype(jnp.int32)


def draw_patch_vertical_bands(key, part):
    return (tile_layout(key) % BANDS_ON_CHIPSET).astype(jnp.int32)


def draw_active_patch_numbers(key, part):
    loaded = jax.random.randint(jax.random.fold_in(key, 21), (N_BLK, N_REP, 1), 0, 4) == 0
    ceiling = jnp.where(loaded, CAP, max(1, CAP // 4))
    counts = jax.random.randint(jax.random.fold_in(key, 22), (N_BLK, N_REP, N_BLK), 0, 2 ** 20) % ceiling + 1
    diagonal = jnp.arange(N_BLK, dtype=jnp.int32)[:, None, None] == jnp.arange(N_BLK, dtype=jnp.int32)[None, None, :]
    return jnp.where(diagonal, CAP, counts).astype(jnp.int32)


def level_of(own_key, dims, cuts, least, top_value):
    def one(dim, shards_of):
        steps = jax.random.uniform(jax.random.fold_in(jax.random.fold_in(own_key, 6), dim), (shards_of,), jnp.float32, least / len(cuts), top_value / len(cuts))
        return jnp.repeat(jnp.exp(steps), dims[dim] // shards_of).reshape((-1,) + (1,) * (len(dims) - dim - 1))

    gain = one(*cuts[0])
    for cut in cuts[1:]:
        gain = gain * one(*cut)
    return gain


def scatter_about(rng, extent, spread, reach, split=(), kind=jnp.bfloat16):
    loudness = level_of(rng, extent, split, -0.22, 0.18) if split else 1.0
    array = jax.random.normal(rng, extent, jnp.float32) * spread * loudness
    return jnp.minimum(jnp.maximum(array, -reach), reach).astype(kind)


def setup_inputs(seed: int = 0) -> dict:
    seeds = jax.random.split(jax.random.key(seed), 8)
    features = scatter_about(seeds[0], (ROWS, F), 1.0, 6.0, ((0, 128),))
    tiles = scatter_about(seeds[1], (N_BLK, N_REP, N_BLK, CAP, BS, BS), (N_BLK * BS * CAP // (4 * BANDS_ON_CHIPSET * N_REP) + BS) ** -0.5, 0.1875, ((0, 32), (1, 4)))
    patch_horizontal_bands = draw_patch_horizontal_bands(jax.random.fold_in(seeds[7], 71), 0)
    patch_vertical_bands = draw_patch_vertical_bands(jax.random.fold_in(seeds[7], 71), 0)
    active_patch_numbers = draw_active_patch_numbers(jax.random.fold_in(seeds[7], 71), 0)
    weight = scatter_about(seeds[5], (F, F), F ** -0.5, 0.375)
    cotangent = scatter_about(seeds[6], (ROWS, F), 1.0, 6.0, ((0, 128),))
    return dict(features=features, tiles=tiles, patch_horizontal_bands=patch_horizontal_bands, patch_vertical_bands=patch_vertical_bands, active_patch_numbers=active_patch_numbers, weight=weight, cotangent=cotangent)


def pick_blocks(blocks, indices):
    return jnp.take(blocks, indices, axis=0)

def reference(features, tiles, patch_horizontal_bands, patch_vertical_bands, active_patch_numbers, weight, cotangent):
    highest = lax.Precision.HIGHEST
    panels = features.reshape(N_BLK, N_REP, BANDS_ON_CHIPSET, BS, F)
    storage_positions_list = jnp.arange(CAP, dtype=jnp.int32)

    def group_sum(horizontal_stripe):
        total = jnp.zeros((BANDS_IN_STRIPE, BS, F), jnp.float32)
        for copy_ordinal in range(N_REP):
            block_tiles = tiles[horizontal_stripe, copy_ordinal]
            source = panels[:, copy_ordinal]
            chosen = jax.vmap(pick_blocks)(source, patch_vertical_bands[horizontal_stripe, copy_ordinal])
            product = jnp.einsum('pkij,pkjf->pkif', block_tiles.astype(jnp.float32), chosen.astype(jnp.float32), precision=highest)
            patch_activity_mask = (storage_positions_list[None, :] < active_patch_numbers[horizontal_stripe, copy_ordinal][:, None]).astype(jnp.float32)
            patch_arrangement = (patch_horizontal_bands[horizontal_stripe, copy_ordinal][:, :, None] == jnp.arange(BANDS_IN_STRIPE, dtype=jnp.int32)[None, None, :]).astype(jnp.float32) * patch_activity_mask[:, :, None]
            total = total + jnp.einsum('pkg,pkif->gif', patch_arrangement, product, precision=highest)
        return total
    summed = lax.map(group_sum, jnp.arange(N_BLK, dtype=jnp.int32))
    aggregated = summed.reshape(ROWS, F).astype(jnp.bfloat16)
    linear = jnp.dot(aggregated, weight, preferred_element_type=jnp.float32)
    output = jax.nn.silu(linear).astype(jnp.bfloat16)
    sigma = jax.nn.sigmoid(linear)
    grad_linear = (cotangent.astype(jnp.float32) * sigma * (1.0 + linear * (1.0 - sigma))).astype(jnp.bfloat16)
    weight_total = lax.dot_general(aggregated, grad_linear, (((0,), (0,)), ((), ())), preferred_element_type=jnp.float32)
    grad_weight = weight_total * jnp.float32(1.0 / math.sqrt(ROWS))
    back = lax.dot_general(grad_linear, weight, (((1,), (1,)), ((), ())), preferred_element_type=jnp.float32).astype(jnp.bfloat16)
    back_groups = back.reshape(N_BLK, BANDS_IN_STRIPE, BS, F)

    def target_sum(destination_submatrix):
        pieces = []
        for copy_ordinal in range(N_REP):
            block_tiles = tiles[:, copy_ordinal, destination_submatrix]
            chosen = jax.vmap(pick_blocks)(back_groups, patch_horizontal_bands[:, copy_ordinal, destination_submatrix])
            product = jnp.einsum('gkji,gkjf->gkif', block_tiles.astype(jnp.float32), chosen.astype(jnp.float32), precision=highest)
            patch_activity_mask = (storage_positions_list[None, :] < active_patch_numbers[:, copy_ordinal, destination_submatrix][:, None]).astype(jnp.float32)
            patch_arrangement = (patch_vertical_bands[:, copy_ordinal, destination_submatrix][:, :, None] == jnp.arange(BANDS_ON_CHIPSET, dtype=jnp.int32)[None, None, :]).astype(jnp.float32) * patch_activity_mask[:, :, None]
            pieces.append(jnp.einsum('gkc,gkif->cif', patch_arrangement, product, precision=highest))
        return jnp.stack(pieces)
    grad_input = lax.map(target_sum, jnp.arange(N_BLK, dtype=jnp.int32)).reshape(ROWS, F)
    return (output, grad_weight, grad_input)
```

```python
import functools
import math

import jax
import jax.numpy as jnp
from jax import lax
from jax.experimental import pallas as pl
from jax.experimental.pallas import tpu as pltpu
from jax.sharding import PartitionSpec as P

MESH = pl.DeviceIdType.MESH
F = 256
BS = 128
CAP = 12
PANELS = 32
PANEL = 512
HALF = 256
QUARTER = 128
SLOTS = PANELS * CAP
bf16 = jnp.bfloat16
f32 = jnp.float32


class Place:
    def __init__(self):
        b = lax.axis_index("blk")
        r = lax.axis_index("rep")
        self.b, self.r = b, r
        self.c = {"x": lax.rem(b, 4), "z": lax.rem(b // 4, 4)}
        self.y = b // 16
        self.yp = 1 - self.y
        self.core = lax.rem(r, 2)
        self.yh = r // 2
        self.nb = {"y": {"blk": self.blk(self.yp, self.c["z"], self.c["x"])}}
        for axis in ("x", "z"):
            for name, step in (("+", 1), ("-", -1), ("2", 2)):
                self.nb[axis + name] = {"blk": self.at(self.y, axis, step, 0)}
        self.nb["core"] = {"rep": self.yh * 2 + 1 - self.core}
        self.nb["yh"] = {"rep": (1 - self.yh) * 2 + self.core}

    def blk(self, y, z, x):
        return y * 16 + z * 4 + x

    def up(self, axis, step):
        return lax.rem(self.c[axis] + step + 4, 4)

    def at(self, y, first, d, e):
        if first == "x":
            return self.blk(y, self.up("z", e), self.up("x", d))
        return self.blk(y, self.up("z", d), self.up("x", e))

    def on_second(self, y, first, d, e):
        if first == "x":
            return self.blk(y, e, self.up("x", d))
        return self.blk(y, self.up("z", d), e)

    def barrier(self, names):
        sem = pltpu.get_barrier_semaphore()
        for name in names:
            pl.semaphore_signal(sem, inc=1, device_id=self.nb[name], device_id_type=MESH)
        pl.semaphore_wait(sem, len(names))


class Sends:
    def __init__(self, place, send, recv):
        self.place, self.send, self.recv = place, send, recv
        self.count = 0
        self.pending = []

    def to(self, where, src, dst):
        t = self.count
        self.count += 1
        copy = pltpu.make_async_remote_copy(
            src, dst, self.send.at[t], self.recv.at[t],
            device_id=self.place.nb[where], device_id_type=MESH,
        )
        copy.start()
        self.pending.append(copy)
        return t

    def wait(self, t, dst):
        pltpu.make_async_remote_copy(
            dst, dst, self.send.at[t], self.recv.at[t],
            device_id=self.place.nb["y"], device_id_type=MESH,
        ).wait_recv()

    def drain(self):
        for copy in self.pending:
            copy.wait_send()


PARTS = (("x", "z", 0), ("z", "x", 1))


def load_tiles(tiles_hbm, tiles, sem):
    copies = [
        pltpu.make_async_copy(
            tiles_hbm.at[pl.ds(i * SLOTS // 4, SLOTS // 4)],
            tiles.at[pl.ds(i * SLOTS // 4, SLOTS // 4)],
            sem.at[i],
        )
        for i in range(4)
    ]
    for copy in copies:
        copy.start()
    return copies


def forward_kernel(
    inv, f_ref, tiles_hbm, w_ref, ct_ref,
    out_ref, gw_ref, bt_ref,
    g, tiles, acc, in1, sbuf, in2, send, recv, loc,
):
    me = Place()
    names = ("x+", "x-", "z+", "z-", "y", "core", "yh")
    me.barrier(names)
    sends = Sends(me, send, recv)
    own = pltpu.make_async_copy(f_ref, g.at[me.b], loc.at[4])
    own.start()

    def rows(blk, lo, n):
        return g.at[blk, pl.ds(lo, n)]

    def push(where, blk, lo, n, mine=False):
        src = f_ref.at[pl.ds(lo, n)] if mine else rows(blk, lo, n)
        return sends.to(where, src, rows(blk, lo, n))

    def arrive(t, blk, lo, n):
        sends.wait(t, rows(blk, lo, n))

    to_y = [push("y", me.b, i * HALF, HALF, True) for i in range(2)]
    p1, p1f, p2, p2f = {}, {}, {}, {}

    def start2(y, s, p, d, mine=False):
        blk = me.at(y, p[0], d, 0)
        lo = p[2] * HALF
        p2[s, p[2], d] = (push(p[1] + "+", blk, lo, HALF, mine), push(p[1] + "-", blk, lo, HALF, mine))

    def stage1(y, s, mine):
        for p in PARTS:
            blk = me.at(y, p[0], 0, 0)
            lo = p[2] * HALF
            p1[s, p[2]] = (push(p[0] + "+", blk, lo, HALF, mine), push(p[0] + "-", blk, lo, HALF, mine))
        for p in PARTS:
            start2(y, s, p, 0, mine)

    def stage2(y, s):
        for p in PARTS:
            lo = p[2] * HALF
            t = p1[s, p[2]]
            arrive(t[0], me.at(y, p[0], -1, 0), lo, HALF)
            f0 = push(p[0] + "+", me.at(y, p[0], -1, 0), lo, QUARTER)
            start2(y, s, p, -1)
            arrive(t[1], me.at(y, p[0], 1, 0), lo, HALF)
            f1 = push(p[0] + "-", me.at(y, p[0], 1, 0), lo + QUARTER, QUARTER)
            start2(y, s, p, 1)
            p1f[s, p[2]] = (f0, f1)

    def stage3(y, s):
        for p in PARTS:
            lo = p[2] * HALF
            f0, f1 = p1f[s, p[2]]
            arrive(f0, me.at(y, p[0], 2, 0), lo, QUARTER)
            arrive(f1, me.at(y, p[0], 2, 0), lo + QUARTER, QUARTER)
            start2(y, s, p, 2)

    def stage4(y, s, d):
        for p in PARTS:
            lo = p[2] * HALF
            t = p2[s, p[2], d]
            arrive(t[0], me.at(y, p[0], d, -1), lo, HALF)
            f0 = push(p[1] + "+", me.at(y, p[0], d, -1), lo, QUARTER)
            arrive(t[1], me.at(y, p[0], d, 1), lo, HALF)
            f1 = push(p[1] + "-", me.at(y, p[0], d, 1), lo + QUARTER, QUARTER)
            p2f[s, p[2], d] = (f0, f1)

    def compute(y, p, d, first=False):
        lo = p[2] * HALF

        @pl.loop(0, 4)
        def _(hg):
            lhs = []
            for e in range(4):
                blk = me.on_second(y, p[0], d, e)
                for v in range(2):
                    base = blk * 64 + hg * 16 + p[2] * 2 + v
                    lhs.append(jnp.concatenate([tiles[inv[base + h * 4]] for h in range(4)], axis=0))
            lhs = jnp.concatenate(lhs, axis=1)
            rhs = jnp.concatenate(
                [g[me.on_second(y, p[0], d, e), pl.ds(lo, HALF), :] for e in range(4)], axis=0
            )
            part = jnp.dot(lhs, rhs, preferred_element_type=f32)
            if first:
                acc[hg] = part
            else:
                acc[hg] += part

    def stage5(y, s, d, first=False):
        for p in PARTS:
            lo = p[2] * HALF
            f0, f1 = p2f[s, p[2], d]
            arrive(f0, me.at(y, p[0], d, 2), lo, QUARTER)
            arrive(f1, me.at(y, p[0], d, 2), lo + QUARTER, QUARTER)
            compute(y, p, d, first and p[2] == 0)

    y, yp = me.y, me.yp
    stage1(y, 0, True)
    loads = load_tiles(tiles_hbm, tiles, loc)
    tiles[SLOTS] = jnp.zeros((BS, BS), bf16)
    twin = me.blk(yp, me.c["z"], me.c["x"])
    for i in range(2):
        arrive(to_y[i], twin, i * HALF, HALF)
    stage2(y, 0)
    stage1(yp, 1, False)
    stage3(y, 0)
    for d in (0, -1, 1):
        stage4(y, 0, d)
    stage2(yp, 1)
    stage4(y, 0, 2)
    stage3(yp, 1)
    own.wait()
    for copy in loads:
        copy.wait()
    stage5(y, 0, 0, True)
    stage4(yp, 1, 0)
    stage5(y, 0, -1)
    stage4(yp, 1, -1)
    stage5(y, 0, 1)
    stage4(yp, 1, 1)
    stage5(y, 0, 2)
    stage4(yp, 1, 2)
    for d in (0, -1, 1, 2):
        stage5(yp, 1, d)

    far = 1 - me.yh
    other = 1 - me.core
    t_far = sends.to("core", acc.at[far * 2 + other], in1.at[far])
    t_near = sends.to("core", acc.at[me.yh * 2 + other], in1.at[me.yh])
    sends.wait(t_far, in1.at[far])
    sbuf[...] = (acc[far * 2 + me.core] + in1[far]).astype(bf16)
    t_yh = sends.to("yh", sbuf, in2)
    sends.wait(t_near, in1.at[me.yh])
    near = acc[me.r] + in1[me.yh]
    acc[me.r] = near
    sends.wait(t_yh, in2)
    agg = (acc[me.r] + in2[...].astype(f32)).astype(bf16)
    linear = jnp.dot(agg, w_ref[...], preferred_element_type=f32)
    sigma = 1.0 / (1.0 + jnp.exp(-linear))
    out_ref[...] = (linear * sigma).astype(bf16)
    gl = (ct_ref[...].astype(f32) * sigma * (1.0 + linear * (1.0 - sigma))).astype(bf16)
    back = lax.dot_general(w_ref[...], gl, (((1,), (1,)), ((), ())), preferred_element_type=f32)
    bt_ref[me.r] = back.astype(bf16)
    b_yh = sends.to("yh", bt_ref.at[me.r], bt_ref.at[me.r])
    b_core = sends.to("core", bt_ref.at[me.r], bt_ref.at[me.r])
    gw_ref[...] = lax.dot_general(agg, gl, (((0,), (0,)), ((), ())), preferred_element_type=f32)
    there = far * 2 + me.core
    sends.wait(b_yh, bt_ref.at[there])
    b_fwd = sends.to("core", bt_ref.at[there], bt_ref.at[there])
    sends.wait(b_core, bt_ref.at[me.yh * 2 + other])
    sends.wait(b_fwd, bt_ref.at[far * 2 + other])
    sends.drain()
    assert sends.count <= 90


def backward_kernel(
    inv, tiles_hbm, bt_ref, gwp_ref,
    gi_ref, gw_ref,
    tiles, pbuf, in_h, in_f, sb, in_h1, in_f1, tb, sy, in_y,
    gx, gz, gb, gacc, send, recv, loc,
):
    me = Place()
    names = ("x+", "x-", "x2", "z+", "z-", "z2", "y", "core", "yh")
    me.barrier(names)
    sends = Sends(me, send, recv)
    loads = load_tiles(tiles_hbm, tiles, loc)
    tiles[SLOTS] = jnp.zeros((BS, BS), bf16)
    D = (2, -1, 1, 0)
    lo, hi = pl.ds(0, QUARTER), pl.ds(QUARTER, QUARTER)
    y, yp = me.y, me.yp
    ys = (y, yp)

    cx, cz = me.c["x"], me.c["z"]

    def piece(axis_x, n, ref):
        return ref.at[pl.ds(axis_x * n, n)]

    hops = ((1, "+"), (2, "2"), (3, "-"))
    t_gx = [
        sends.to("x" + name, piece(me.up("x", step), 64, gwp_ref), gx.at[i])
        for i, (step, name) in enumerate(hops)
    ]
    gstate = {}

    def gw_step(n):
        if n == 0:
            total = gwp_ref[pl.ds(cx * 64, 64), :]
            for i in range(3):
                sends.wait(t_gx[i], gx.at[i])
                total = total + gx[i]
            gacc[0] = total
            gstate["z"] = [
                sends.to("z" + name, gacc.at[0, pl.ds(me.up("z", step) * 16, 16)], gz.at[i])
                for i, (step, name) in enumerate(hops)
            ]
        elif n == 1:
            total = gacc[0, pl.ds(cz * 16, 16), :]
            for i in range(3):
                sends.wait(gstate["z"][i], gz.at[i])
                total = total + gz[i]
            gb[0] = total
            gstate["b"] = sends.to("core", gb.at[0], gb.at[3])
        elif n in (2, 3):
            sends.wait(gstate["b"], gb.at[n + 1])
            gb[n - 1] = gb[n - 2] + gb[n + 1]
            gstate["b"] = sends.to(("yh", "y")[n - 2], gb.at[n - 1], gb.at[n + 2])
        elif n == 4:
            sends.wait(gstate["b"], gb.at[5])
            gacc[1, pl.ds(cz * 16, 16), :] = (gb[2] + gb[5]) * f32(1.0 / math.sqrt(65536))
            mine = gacc.at[1, pl.ds(cz * 16, 16)]
            gstate["az"] = [sends.to("z" + name, mine, mine) for _, name in hops]
        elif n == 5:
            for i, (step, _) in enumerate(hops):
                sends.wait(gstate["az"][i], gacc.at[1, pl.ds(me.up("z", -step) * 16, 16)])
            gw_ref[pl.ds(cx * 64, 64), :] = gacc[1]
            mine = piece(cx, 64, gw_ref)
            gstate["ax"] = [sends.to("x" + name, mine, mine) for _, name in hops]
        else:
            for i, (step, _) in enumerate(hops):
                sends.wait(gstate["ax"][i], piece(me.up("x", -step), 64, gw_ref))

    for copy in loads:
        copy.wait()

    slot = {}
    for s in (1, 0):
        for k, d in enumerate(D):
            for p in PARTS:
                slot[s, d, p[2]] = (s * 4 + k) * 2 + p[2]

    E = (2, 1, 3, 0)
    halves, fulls, halves1, fulls1 = {}, {}, {}, {}

    def compute(s, d, p):
        q = slot[s, d, p[2]]

        @pl.loop(0, 4)
        def _(e):
            blk = me.at(ys[s], p[0], d, e)
            rhs = []
            for h in range(16):
                base = blk * 64 + h * 4 + p[2] * 2
                rhs.append(jnp.concatenate([tiles[inv[base]], tiles[inv[base + 1]]], axis=1))
            rhs = jnp.concatenate(rhs, axis=0)
            lhs = jnp.concatenate([bt_ref[i] for i in range(4)], axis=1)
            pbuf[q, e] = jnp.dot(lhs, rhs, preferred_element_type=f32).astype(bf16)

        halves[q] = (
            sends.to(p[1] + "+", pbuf.at[q, 2, lo], in_h.at[q, 0]),
            sends.to(p[1] + "-", pbuf.at[q, 2, hi], in_h.at[q, 1]),
        )

    def second(s, d, p):
        q = slot[s, d, p[2]]
        t = halves[q]
        sends.wait(t[0], in_h.at[q, 0])
        pbuf[q, 1, lo, :] = (pbuf[q, 1, lo, :].astype(f32) + in_h[q, 0].astype(f32)).astype(bf16)
        up = sends.to(p[1] + "+", pbuf.at[q, 1], in_f.at[q, 0])
        sends.wait(t[1], in_h.at[q, 1])
        pbuf[q, 3, hi, :] = (pbuf[q, 3, hi, :].astype(f32) + in_h[q, 1].astype(f32)).astype(bf16)
        down = sends.to(p[1] + "-", pbuf.at[q, 3], in_f.at[q, 1])
        fulls[q] = (up, down)

    def third(s, d, p):
        q = slot[s, d, p[2]]
        t = fulls[q]
        u = s * 2 + p[2]
        sends.wait(t[0], in_f.at[q, 0])
        sends.wait(t[1], in_f.at[q, 1])
        total = pbuf[q, 0].astype(f32) + in_f[q, 0].astype(f32) + in_f[q, 1].astype(f32)
        if d == 2:
            sb[u, 0] = total.astype(bf16)
            halves1[u] = (
                sends.to(p[0] + "+", sb.at[u, 0, lo], in_h1.at[u, 0]),
                sends.to(p[0] + "-", sb.at[u, 0, hi], in_h1.at[u, 1]),
            )
        elif d == 1:
            sb[u, 1] = total.astype(bf16)
            sends.wait(halves1[u][0], in_h1.at[u, 0])
            sb[u, 1, lo, :] = (total[:QUARTER] + in_h1[u, 0].astype(f32)).astype(bf16)
            fulls1[u, 0] = sends.to(p[0] + "+", sb.at[u, 1], in_f1.at[u, 0])
        elif d == -1:
            sb[u, 2] = total.astype(bf16)
            sends.wait(halves1[u][1], in_h1.at[u, 1])
            sb[u, 2, hi, :] = (total[QUARTER:] + in_h1[u, 1].astype(f32)).astype(bf16)
            fulls1[u, 1] = sends.to(p[0] + "-", sb.at[u, 2], in_f1.at[u, 1])
        else:
            tb[p[2]] = total

    to_y = {}

    def fourth(s, p):
        u = s * 2 + p[2]
        for i in range(2):
            sends.wait(fulls1[u, i], in_f1.at[u, i])
        total = tb[p[2]] + in_f1[u, 0].astype(f32) + in_f1[u, 1].astype(f32)
        if s == 1:
            sy[p[2]] = total.astype(bf16)
            to_y[p[2]] = sends.to("y", sy.at[p[2]], in_y.at[p[2]])
        else:
            sends.wait(to_y[p[2]], in_y.at[p[2]])
            total = total + in_y[p[2]].astype(f32)
            gi_ref[pl.ds(p[2] * HALF, HALF), :] = total.T

    steps = [(s, d) for s in (1, 0) for d in D]
    n = len(steps)

    def both(fn, step):
        for p in PARTS:
            fn(*step, p)

    for i in range(n + 2):
        if i < n:
            both(compute, steps[i])
        if 1 <= i <= n:
            both(second, steps[i - 1])
        if i >= 2:
            both(third, steps[i - 2])
            if i - 2 == 3:
                for p in PARTS:
                    fourth(1, p)
        if 1 <= i <= 7:
            gw_step(i - 1)
    for p in PARTS:
        fourth(0, p)
    sends.drain()
    assert sends.count <= 110


def inverse(bands, cols, counts):
    slots = jnp.arange(CAP, dtype=jnp.int32)
    where = jnp.where(slots[None] < counts[:, None], bands * 4 + cols, -1)
    ids = jnp.arange(SLOTS, dtype=jnp.int32).reshape(PANELS, CAP) - SLOTS
    hit = where[:, None, :] == jnp.arange(64, dtype=jnp.int32)[None, :, None]
    return (jnp.sum(jnp.where(hit, ids[:, None, :], 0), axis=2) + SLOTS).reshape(-1)


def local(features, tiles, bands, cols, counts, weight, cotangent):
    inv = inverse(bands[0, 0], cols[0, 0], counts[0, 0])
    tiles = tiles.reshape(SLOTS, BS, BS)
    vmem = pl.BlockSpec(memory_space=pltpu.VMEM)
    hbm = pl.BlockSpec(memory_space=pl.ANY)
    smem = pl.BlockSpec(memory_space=pltpu.SMEM)
    dma = pltpu.SemaphoreType.DMA
    output, gw_part, back = pl.pallas_call(
        forward_kernel,
        out_shape=(
            jax.ShapeDtypeStruct((PANEL, F), bf16),
            jax.ShapeDtypeStruct((F, F), f32),
            jax.ShapeDtypeStruct((4, F, PANEL), bf16),
        ),
        in_specs=[smem, vmem, hbm, vmem, vmem],
        out_specs=(vmem, vmem, vmem),
        scratch_shapes=[
            pltpu.VMEM((PANELS, PANEL, F), bf16),
            pltpu.VMEM((SLOTS + 1, BS, BS), bf16),
            pltpu.VMEM((4, PANEL, F), f32),
            pltpu.VMEM((2, PANEL, F), f32),
            pltpu.VMEM((PANEL, F), bf16),
            pltpu.VMEM((PANEL, F), bf16),
            dma((90,)), dma((90,)), dma((5,)),
        ],
        compiler_params=pltpu.CompilerParams(
            collective_id=0, has_side_effects=True, vmem_limit_bytes=56 * 2**20
        ),
        name="gather_forward",
    )(inv, features, tiles, weight, cotangent)
    grad_input, grad_weight = pl.pallas_call(
        backward_kernel,
        out_shape=(
            jax.ShapeDtypeStruct((PANEL, F), f32),
            jax.ShapeDtypeStruct((F, F), f32),
        ),
        in_specs=[smem, hbm, vmem, vmem],
        out_specs=(vmem, vmem),
        scratch_shapes=[
            pltpu.VMEM((SLOTS + 1, BS, BS), bf16),
            pltpu.VMEM((16, 4, F, HALF), bf16),
            pltpu.VMEM((16, 2, QUARTER, HALF), bf16),
            pltpu.VMEM((16, 2, F, HALF), bf16),
            pltpu.VMEM((4, 3, F, HALF), bf16),
            pltpu.VMEM((4, 2, QUARTER, HALF), bf16),
            pltpu.VMEM((4, 2, F, HALF), bf16),
            pltpu.VMEM((2, F, HALF), f32),
            pltpu.VMEM((2, F, HALF), bf16),
            pltpu.VMEM((2, F, HALF), bf16),
            pltpu.VMEM((3, 64, F), f32),
            pltpu.VMEM((3, 16, F), f32),
            pltpu.VMEM((6, 16, F), f32),
            pltpu.VMEM((2, 64, F), f32),
            dma((110,)), dma((110,)), dma((4,)),
        ],
        compiler_params=pltpu.CompilerParams(
            collective_id=1, has_side_effects=True, vmem_limit_bytes=56 * 2**20
        ),
        name="backward_scatter",
    )(inv, tiles, back, gw_part)
    return output, grad_weight, grad_input


def solution(mesh):
    placed = (
        P(("blk", "rep"), None),
        P("blk", "rep", None, None, None, None),
        P("blk", "rep", None, None),
        P("blk", "rep", None, None),
        P("blk", "rep", None),
        P(),
        P(("blk", "rep"), None),
    )
    return jax.shard_map(
        local,
        mesh=mesh,
        in_specs=placed,
        out_specs=(P(("blk", "rep"), None), P(), P(("blk", "rep"), None)),
        check_vma=False,
    )
```

```python
import functools
import math

import jax
import jax.numpy as jnp
from jax import lax
from jax.experimental import pallas as pl
from jax.experimental.pallas import tpu as pltpu
from jax.sharding import PartitionSpec as P

MESH = pl.DeviceIdType.MESH
F = 256
BS = 128
CAP = 12
PANELS = 32
PANEL = 512
HALF = 256
QUARTER = 128
SLOTS = PANELS * CAP
SENDS = 200
bf16 = jnp.bfloat16
f32 = jnp.float32


class Place:
    def __init__(self):
        b = lax.axis_index("blk")
        r = lax.axis_index("rep")
        self.b, self.r = b, r
        self.c = {"x": lax.rem(b, 4), "z": lax.rem(b // 4, 4)}
        self.y = b // 16
        self.yp = 1 - self.y
        self.core = lax.rem(r, 2)
        self.yh = r // 2
        self.nb = {"y": {"blk": self.blk(self.yp, self.c["z"], self.c["x"])}}
        for axis in ("x", "z"):
            for name, step in (("+", 1), ("-", -1), ("2", 2)):
                self.nb[axis + name] = {"blk": self.at(self.y, axis, step, 0)}
        self.nb["core"] = {"rep": self.yh * 2 + 1 - self.core}
        self.nb["yh"] = {"rep": (1 - self.yh) * 2 + self.core}

    def blk(self, y, z, x):
        return y * 16 + z * 4 + x

    def up(self, axis, step):
        return lax.rem(self.c[axis] + step + 4, 4)

    def at(self, y, first, d, e):
        if first == "x":
            return self.blk(y, self.up("z", e), self.up("x", d))
        return self.blk(y, self.up("z", d), self.up("x", e))

    def on_second(self, y, first, d, e):
        if first == "x":
            return self.blk(y, e, self.up("x", d))
        return self.blk(y, self.up("z", d), e)

    def barrier(self, names):
        sem = pltpu.get_barrier_semaphore()
        for name in names:
            pl.semaphore_signal(sem, inc=1, device_id=self.nb[name], device_id_type=MESH)
        pl.semaphore_wait(sem, len(names))


class Sends:
    def __init__(self, place, send, recv):
        self.place, self.send, self.recv = place, send, recv
        self.count = 0
        self.pending = []

    def to(self, where, src, dst):
        t = self.count
        self.count += 1
        copy = pltpu.make_async_remote_copy(
            src, dst, self.send.at[t], self.recv.at[t],
            device_id=self.place.nb[where], device_id_type=MESH,
        )
        copy.start()
        self.pending.append(copy)
        return t

    def wait(self, t, dst):
        pltpu.make_async_remote_copy(
            dst, dst, self.send.at[t], self.recv.at[t],
            device_id=self.place.nb["y"], device_id_type=MESH,
        ).wait_recv()

    def drain(self):
        for copy in self.pending:
            copy.wait_send()


PARTS = (("x", "z", 0), ("z", "x", 1))


def load_tiles(tiles_hbm, tiles, sem):
    copies = [
        pltpu.make_async_copy(
            tiles_hbm.at[pl.ds(i * SLOTS // 4, SLOTS // 4)],
            tiles.at[pl.ds(i * SLOTS // 4, SLOTS // 4)],
            sem.at[i],
        )
        for i in range(4)
    ]
    for copy in copies:
        copy.start()
    return copies


def kernel(
    inv, f_ref, tiles_hbm, w_ref, ct_ref,
    out_ref, gi_ref, gw_ref,
    g, tiles, acc, in1, sbuf, in2, bt, gwp,
    pbuf, in_h, in_f, in_e, sb, in_h1, in_f1, tb, sy, in_y,
    gx, gz, gb, gacc, send, recv, loc,
):
    me = Place()
    me.barrier(("x+", "x-", "x2", "z+", "z-", "z2", "y", "core", "yh"))
    sends = Sends(me, send, recv)
    y, yp = me.y, me.yp
    ys = (y, yp)

    def rows(blk, lo, n):
        return g.at[blk, pl.ds(lo, n)]

    def push(where, blk, lo, n, mine=False):
        src = f_ref.at[pl.ds(lo, n)] if mine else rows(blk, lo, n)
        return sends.to(where, src, rows(blk, lo, n))

    def arrive(t, blk, lo, n):
        sends.wait(t, rows(blk, lo, n))

    p1, p1f, p2, p2f, far2 = {}, {}, {}, {}, {}

    def start2(s, p, d, mine=False):
        blk = me.at(ys[s], p[0], d, 0)
        lo = p[2] * HALF
        p2[s, p[2], d] = (push(p[1] + "+", blk, lo, HALF, mine), push(p[1] + "-", blk, lo, HALF, mine))

    def stage1(s, mine):
        for p in PARTS:
            blk = me.at(ys[s], p[0], 0, 0)
            lo = p[2] * HALF
            p1[s, p[2]] = (push(p[0] + "+", blk, lo, HALF, mine), push(p[0] + "-", blk, lo, HALF, mine))
        for p in PARTS:
            start2(s, p, 0, mine)

    def stage2(s):
        for p in PARTS:
            lo = p[2] * HALF
            t = p1[s, p[2]]
            at = functools.partial(me.at, ys[s], p[0])
            arrive(t[0], at(-1, 0), lo, HALF)
            f0 = push(p[0] + "+", at(-1, 0), lo, QUARTER)
            start2(s, p, -1)
            arrive(t[1], at(1, 0), lo, HALF)
            f1 = push(p[0] + "-", at(1, 0), lo + QUARTER, QUARTER)
            start2(s, p, 1)
            p1f[s, p[2]] = (f0, f1)

    def stage3(s):
        for p in PARTS:
            lo = p[2] * HALF
            f0, f1 = p1f[s, p[2]]
            arrive(f0, me.at(ys[s], p[0], 2, 0), lo, QUARTER)
            arrive(f1, me.at(ys[s], p[0], 2, 0), lo + QUARTER, QUARTER)
            start2(s, p, 2)

    def stage4(s, d):
        for p in PARTS:
            lo = p[2] * HALF
            t = p2[s, p[2], d]
            at = functools.partial(me.at, ys[s], p[0])
            arrive(t[0], at(d, -1), lo, HALF)
            if s == 0:
                f0 = push(p[1] + "+", at(d, -1), lo, QUARTER)
            arrive(t[1], at(d, 1), lo, HALF)
            if s == 0:
                p2f[p[2], d] = (f0, push(p[1] + "-", at(d, 1), lo + QUARTER, QUARTER))

    def stage5(d):
        for p in PARTS:
            lo = p[2] * HALF
            f0, f1 = p2f[p[2], d]
            blk = me.at(y, p[0], d, 2)
            arrive(f0, blk, lo, QUARTER)
            arrive(f1, blk, lo + QUARTER, QUARTER)
            far2[p[2], d] = push("y", blk, lo, HALF)

    def stage6(d):
        for p in PARTS:
            arrive(far2[p[2], d], me.at(yp, p[0], d, 2), p[2] * HALF, HALF)

    def product(hg, s, p, panels):
        lo = p[2] * HALF
        blks = [me.at(ys[s], p[0], d, e) for d, e in panels]
        lhs = []
        for blk in blks:
            for v in range(2):
                base = blk * 64 + hg * 16 + p[2] * 2 + v
                lhs.append(jnp.concatenate([tiles[inv[base + h * 4]] for h in range(4)], axis=0))
        lhs = jnp.concatenate(lhs, axis=1)
        rhs = jnp.concatenate([g[blk, pl.ds(lo, HALF), :] for blk in blks], axis=0)
        return jnp.dot(lhs, rhs, preferred_element_type=f32)

    def compute(s, k, panels, first=False):
        p = PARTS[k]

        @pl.loop(0, 4)
        def _(hg):
            if first:
                acc[hg] = product(hg, s, p, panels)
            else:
                acc[hg] += product(hg, s, p, panels)

    line = ((0, 0), (-1, 0), (1, 0), (2, 0))
    near = ((0, -1), (0, 1), (-1, -1), (-1, 1))
    apart = ((1, -1), (1, 1), (2, -1), (2, 1))
    across = ((0, 2), (-1, 2), (1, 2), (2, 2))

    stage1(0, True)
    to_y = [push("y", me.b, i * HALF, HALF, True) for i in range(2)]
    own = pltpu.make_async_copy(f_ref, g.at[me.b], loc.at[4])
    own.start()
    loads = load_tiles(tiles_hbm, tiles, loc)
    tiles[SLOTS] = jnp.zeros((BS, BS), bf16)
    stage2(0)
    twin = me.blk(yp, me.c["z"], me.c["x"])
    for i in range(2):
        arrive(to_y[i], twin, i * HALF, HALF)
    stage1(1, False)
    stage3(0)
    own.wait()
    for copy in loads:
        copy.wait()
    compute(0, 0, line, True)
    stage2(1)
    compute(0, 1, line)
    stage4(0, 0)
    stage4(0, -1)
    stage3(1)
    compute(0, 0, near)
    stage4(0, 1)
    compute(0, 1, near)
    stage4(0, 2)
    stage5(0)
    compute(1, 0, line)
    stage5(-1)
    compute(1, 1, line)
    stage5(1)
    compute(0, 0, apart)
    stage5(2)
    compute(0, 1, apart)
    compute(0, 0, across)
    compute(0, 1, across)
    stage4(1, 0)
    stage4(1, -1)
    compute(1, 0, near)
    compute(1, 1, near)
    stage4(1, 1)
    stage4(1, 2)
    compute(1, 0, apart)
    compute(1, 1, apart)
    for d in (0, -1, 1, 2):
        stage6(d)

    far = 1 - me.yh
    other = 1 - me.core

    def last(owner):
        @pl.loop(0, 2)
        def _(i):
            hg = owner * 2 + lax.rem(other + i, 2)
            acc[hg] += product(hg, 1, PARTS[0], across)
            acc[hg] += product(hg, 1, PARTS[1], across)

    last(far)
    t_far = sends.to("core", acc.at[far * 2 + other], in1.at[far])
    last(me.yh)
    t_near = sends.to("core", acc.at[me.yh * 2 + other], in1.at[me.yh])
    sends.wait(t_far, in1.at[far])
    t_yh = []
    for i in range(2):
        part = pl.ds(i * HALF, HALF)
        sbuf[i] = (acc[far * 2 + me.core, part, :] + in1[far, part, :]).astype(bf16)
        t_yh.append(sends.to("yh", sbuf.at[i], in2.at[i]))
    sends.wait(t_near, in1.at[me.yh])
    acc[me.r] += in1[me.yh]
    t_bt = []
    for i in range(2):
        part = pl.ds(i * HALF, HALF)
        sends.wait(t_yh[i], in2.at[i])
        agg = (acc[me.r, part, :] + in2[i].astype(f32)).astype(bf16)
        linear = jnp.dot(agg, w_ref[...], preferred_element_type=f32)
        sigma = 1.0 / (1.0 + jnp.exp(-linear))
        gl = (ct_ref[part, :].astype(f32) * sigma * (1.0 + linear * (1.0 - sigma))).astype(bf16)
        back = lax.dot_general(w_ref[...], gl, (((1,), (1,)), ((), ())), preferred_element_type=f32)
        mine = bt.at[me.r * 2 + i]
        bt[me.r * 2 + i] = back.astype(bf16)
        t_bt.append((sends.to("yh", mine, mine), sends.to("core", mine, mine)))
        out_ref[part, :] = (linear * sigma).astype(bf16)
        local_gw = lax.dot_general(agg, gl, (((0,), (0,)), ((), ())), preferred_element_type=f32)
        if i == 0:
            gwp[...] = local_gw
        else:
            gwp[...] += local_gw

    cx, cz = me.c["x"], me.c["z"]

    def piece(axis_x, n, ref):
        return ref.at[pl.ds(axis_x * n, n)]

    hops = ((1, "+"), (2, "2"), (3, "-"))
    gstate = {}

    def gw_step(n):
        if n == 0:
            gstate["x"] = [
                sends.to("x" + name, piece(me.up("x", step), 64, gwp), gx.at[i])
                for i, (step, name) in enumerate(hops)
            ]
        elif n == 1:
            total = gwp[pl.ds(cx * 64, 64), :]
            for i in range(3):
                sends.wait(gstate["x"][i], gx.at[i])
                total = total + gx[i]
            gacc[0] = total
            gstate["z"] = [
                sends.to("z" + name, gacc.at[0, pl.ds(me.up("z", step) * 16, 16)], gz.at[i])
                for i, (step, name) in enumerate(hops)
            ]
        elif n == 2:
            total = gacc[0, pl.ds(cz * 16, 16), :]
            for i in range(3):
                sends.wait(gstate["z"][i], gz.at[i])
                total = total + gz[i]
            gb[0] = total
            gstate["b"] = sends.to("core", gb.at[0], gb.at[3])
        elif n in (3, 4):
            k = n - 3
            sends.wait(gstate["b"], gb.at[k + 3])
            gb[k + 1] = gb[k] + gb[k + 3]
            gstate["b"] = sends.to(("yh", "y")[k], gb.at[k + 1], gb.at[k + 4])
        elif n == 5:
            sends.wait(gstate["b"], gb.at[5])
            gacc[1, pl.ds(cz * 16, 16), :] = (gb[2] + gb[5]) * f32(1.0 / math.sqrt(65536))
            mine = gacc.at[1, pl.ds(cz * 16, 16)]
            gstate["az"] = [sends.to("z" + name, mine, mine) for _, name in hops]
        elif n == 6:
            for i, (step, _) in enumerate(hops):
                sends.wait(gstate["az"][i], gacc.at[1, pl.ds(me.up("z", -step) * 16, 16)])
            gw_ref[pl.ds(cx * 64, 64), :] = gacc[1]
            mine = piece(cx, 64, gw_ref)
            gstate["ax"] = [sends.to("x" + name, mine, mine) for _, name in hops]
        else:
            for i, (step, _) in enumerate(hops):
                sends.wait(gstate["ax"][i], piece(me.up("x", -step), 64, gw_ref))

    there = far * 2 + me.core
    b_fwd = []
    for i in range(2):
        src = bt.at[there * 2 + i]
        sends.wait(t_bt[i][0], src)
        b_fwd.append(sends.to("core", src, src))
    for i in range(2):
        sends.wait(t_bt[i][1], bt.at[(me.yh * 2 + other) * 2 + i])
        sends.wait(b_fwd[i], bt.at[(far * 2 + other) * 2 + i])

    D = (2, -1, 1, 0)
    lo, hi = pl.ds(0, QUARTER), pl.ds(QUARTER, QUARTER)
    halves, fulls, halves1, fulls1, to_e = {}, {}, {}, {}, {}

    def slot(s, d, p):
        return (s * 4 + D.index(d)) * 2 + p[2]

    def wide(ref, *at):
        return ref[at].astype(f32)

    def spread(s, d, p):
        q = slot(s, d, p)

        @pl.loop(0, 4)
        def _(e):
            blk = me.at(ys[s], p[0], d, e)
            rhs = []
            for h in range(16):
                base = blk * 64 + h * 4 + p[2] * 2
                rhs.append(jnp.concatenate([tiles[inv[base]], tiles[inv[base + 1]]], axis=1))
            rhs = jnp.concatenate(rhs, axis=0)
            lhs = jnp.concatenate([bt[i] for i in range(8)], axis=1)
            pbuf[q, e] = jnp.dot(lhs, rhs, preferred_element_type=f32).astype(bf16)

        u = slot(0, d, p)
        if s == 1:
            fulls[q] = (
                sends.to(p[1] + "+", pbuf.at[q, 1], in_f.at[q, 0]),
                sends.to(p[1] + "-", pbuf.at[q, 3], in_f.at[q, 1]),
            )
            to_e[u] = sends.to("y", pbuf.at[q, 2], in_e.at[u])
        else:
            sends.wait(to_e[u], in_e.at[u])
            pbuf[q, 2] = (wide(pbuf, q, 2) + wide(in_e, u)).astype(bf16)
            halves[q] = (
                sends.to(p[1] + "+", pbuf.at[q, 2, lo], in_h.at[q, 0]),
                sends.to(p[1] + "-", pbuf.at[q, 2, hi], in_h.at[q, 1]),
            )

    def second(s, d, p):
        if s == 1:
            return
        q = slot(s, d, p)
        t = halves[q]
        sends.wait(t[0], in_h.at[q, 0])
        pbuf[q, 1, lo, :] = (pbuf[q, 1, lo, :].astype(f32) + wide(in_h, q, 0)).astype(bf16)
        up = sends.to(p[1] + "+", pbuf.at[q, 1], in_f.at[q, 0])
        sends.wait(t[1], in_h.at[q, 1])
        pbuf[q, 3, hi, :] = (pbuf[q, 3, hi, :].astype(f32) + wide(in_h, q, 1)).astype(bf16)
        down = sends.to(p[1] + "-", pbuf.at[q, 3], in_f.at[q, 1])
        fulls[q] = (up, down)

    def third(s, d, p):
        q = slot(s, d, p)
        t = fulls[q]
        u = s * 2 + p[2]
        sends.wait(t[0], in_f.at[q, 0])
        sends.wait(t[1], in_f.at[q, 1])
        total = wide(pbuf, q, 0) + wide(in_f, q, 0) + wide(in_f, q, 1)
        if d == 2:
            sb[u, 0] = total.astype(bf16)
            halves1[u] = (
                sends.to(p[0] + "+", sb.at[u, 0, lo], in_h1.at[u, 0]),
                sends.to(p[0] + "-", sb.at[u, 0, hi], in_h1.at[u, 1]),
            )
        elif d == 1:
            sb[u, 1] = total.astype(bf16)
            sends.wait(halves1[u][0], in_h1.at[u, 0])
            sb[u, 1, lo, :] = (total[:QUARTER] + wide(in_h1, u, 0)).astype(bf16)
            fulls1[u, 0] = sends.to(p[0] + "+", sb.at[u, 1], in_f1.at[u, 0])
        elif d == -1:
            sb[u, 2] = total.astype(bf16)
            sends.wait(halves1[u][1], in_h1.at[u, 1])
            sb[u, 2, hi, :] = (total[QUARTER:] + wide(in_h1, u, 1)).astype(bf16)
            fulls1[u, 1] = sends.to(p[0] + "-", sb.at[u, 2], in_f1.at[u, 1])
        else:
            tb[p[2]] = total

    home = {}

    def fourth(s, p):
        u = s * 2 + p[2]
        for i in range(2):
            sends.wait(fulls1[u, i], in_f1.at[u, i])
        total = tb[p[2]] + wide(in_f1, u, 0) + wide(in_f1, u, 1)
        if s == 1:
            sy[p[2]] = total.astype(bf16)
            home[p[2]] = sends.to("y", sy.at[p[2]], in_y.at[p[2]])
        else:
            sends.wait(home[p[2]], in_y.at[p[2]])
            total = total + wide(in_y, p[2])
            gi_ref[pl.ds(p[2] * HALF, HALF), :] = total.T

    steps = [(s, d) for s in (1, 0) for d in D]
    n = len(steps)

    def both(fn, step):
        for p in PARTS:
            fn(*step, p)

    for i in range(n + 2):
        if i < n:
            both(spread, steps[i])
        if 1 <= i <= n:
            both(second, steps[i - 1])
        if i >= 2:
            both(third, steps[i - 2])
            if i - 2 == 3:
                for p in PARTS:
                    fourth(1, p)
        if i <= 7:
            gw_step(i)
    for p in PARTS:
        fourth(0, p)
    sends.drain()
    assert sends.count <= SENDS


def copy_kernel(*refs):
    k = len(refs) // 2
    for i in range(k):
        refs[k + i][...] = refs[i][...]


def inverse(bands, cols, counts):
    slots = jnp.arange(CAP, dtype=jnp.int32)
    where = jnp.where(slots[None] < counts[:, None], bands * 4 + cols, -1)
    ids = jnp.arange(SLOTS, dtype=jnp.int32).reshape(PANELS, CAP) - SLOTS
    hit = where[:, None, :] == jnp.arange(64, dtype=jnp.int32)[None, :, None]
    return (jnp.sum(jnp.where(hit, ids[:, None, :], 0), axis=2) + SLOTS).reshape(-1)


def local(features, tiles, bands, cols, counts, weight, cotangent):
    inv = inverse(bands[0, 0], cols[0, 0], counts[0, 0])
    tiles = tiles.reshape(SLOTS, BS, BS)
    vmem = pl.BlockSpec(memory_space=pltpu.VMEM)
    hbm = pl.BlockSpec(memory_space=pl.ANY)
    smem = pl.BlockSpec(memory_space=pltpu.SMEM)
    dma = pltpu.SemaphoreType.DMA
    results = (
        jax.ShapeDtypeStruct((PANEL, F), bf16),
        jax.ShapeDtypeStruct((PANEL, F), f32),
        jax.ShapeDtypeStruct((F, F), f32),
    )
    results = pl.pallas_call(
        kernel,
        out_shape=results,
        in_specs=[smem, vmem, hbm, vmem, vmem],
        out_specs=(vmem, vmem, vmem),
        scratch_shapes=[
            pltpu.VMEM((PANELS, PANEL, F), bf16),
            pltpu.VMEM((SLOTS + 1, BS, BS), bf16),
            pltpu.VMEM((4, PANEL, F), f32),
            pltpu.VMEM((2, PANEL, F), f32),
            pltpu.VMEM((2, HALF, F), bf16),
            pltpu.VMEM((2, HALF, F), bf16),
            pltpu.VMEM((8, F, HALF), bf16),
            pltpu.VMEM((F, F), f32),
            pltpu.VMEM((16, 4, F, HALF), bf16),
            pltpu.VMEM((8, 2, QUARTER, HALF), bf16),
            pltpu.VMEM((16, 2, F, HALF), bf16),
            pltpu.VMEM((8, F, HALF), bf16),
            pltpu.VMEM((4, 3, F, HALF), bf16),
            pltpu.VMEM((4, 2, QUARTER, HALF), bf16),
            pltpu.VMEM((4, 2, F, HALF), bf16),
            pltpu.VMEM((2, F, HALF), f32),
            pltpu.VMEM((2, F, HALF), bf16),
            pltpu.VMEM((2, F, HALF), bf16),
            pltpu.VMEM((3, 64, F), f32),
            pltpu.VMEM((3, 16, F), f32),
            pltpu.VMEM((6, 16, F), f32),
            pltpu.VMEM((2, 64, F), f32),
            dma((SENDS,)), dma((SENDS,)), dma((5,)),
        ],
        compiler_params=pltpu.CompilerParams(
            collective_id=0, has_side_effects=True, vmem_limit_bytes=58 * 2**20
        ),
        name="graph_layer",
    )(inv, features, tiles, weight, cotangent)
    output, grad_input, grad_weight = pl.pallas_call(
        copy_kernel,
        out_shape=tuple(jax.ShapeDtypeStruct(x.shape, x.dtype) for x in results),
        in_specs=[vmem] * 3,
        out_specs=(vmem,) * 3,
        name="results",
    )(*results)
    return output, grad_weight, grad_input


def solution(mesh):
    placed = (
        P(("blk", "rep"), None),
        P("blk", "rep", None, None, None, None),
        P("blk", "rep", None, None),
        P("blk", "rep", None, None),
        P("blk", "rep", None),
        P(),
        P(("blk", "rep"), None),
    )
    return jax.shard_map(
        local,
        mesh=mesh,
        in_specs=placed,
        out_specs=(P(("blk", "rep"), None), P(), P(("blk", "rep"), None)),
        check_vma=False,
    )
```

```python
import functools
import math

import jax
import jax.numpy as jnp
from jax import lax
from jax.experimental import pallas as pl
from jax.experimental.pallas import tpu as pltpu
from jax.sharding import PartitionSpec as P

MESH = pl.DeviceIdType.MESH
F = 256
BS = 128
CAP = 12
PANELS = 32
PANEL = 512
HALF = 256
QUARTER = 128
SLOTS = PANELS * CAP
SENDS = 200
bf16 = jnp.bfloat16
f32 = jnp.float32


class Place:
    def __init__(self):
        b = lax.axis_index("blk")
        r = lax.axis_index("rep")
        self.b, self.r = b, r
        self.c = {"x": lax.rem(b, 4), "z": lax.rem(b // 4, 4)}
        self.y = b // 16
        self.yp = 1 - self.y
        self.core = lax.rem(r, 2)
        self.yh = r // 2
        self.nb = {"y": {"blk": self.blk(self.yp, self.c["z"], self.c["x"])}}
        for axis in ("x", "z"):
            for name, step in (("+", 1), ("-", -1), ("2", 2)):
                self.nb[axis + name] = {"blk": self.at(self.y, axis, step, 0)}
        self.nb["core"] = {"rep": self.yh * 2 + 1 - self.core}
        self.nb["yh"] = {"rep": (1 - self.yh) * 2 + self.core}

    def blk(self, y, z, x):
        return y * 16 + z * 4 + x

    def up(self, axis, step):
        return lax.rem(self.c[axis] + step + 4, 4)

    def at(self, y, first, d, e):
        if first == "x":
            return self.blk(y, self.up("z", e), self.up("x", d))
        return self.blk(y, self.up("z", d), self.up("x", e))

    def on_second(self, y, first, d, e):
        if first == "x":
            return self.blk(y, e, self.up("x", d))
        return self.blk(y, self.up("z", d), e)

    def barrier(self, names):
        sem = pltpu.get_barrier_semaphore()
        for name in names:
            pl.semaphore_signal(sem, inc=1, device_id=self.nb[name], device_id_type=MESH)
        pl.semaphore_wait(sem, len(names))


class Sends:
    def __init__(self, place, send, recv):
        self.place, self.send, self.recv = place, send, recv
        self.count = 0
        self.pending = []

    def to(self, where, src, dst):
        t = self.count
        self.count += 1
        copy = pltpu.make_async_remote_copy(
            src, dst, self.send.at[t], self.recv.at[t],
            device_id=self.place.nb[where], device_id_type=MESH,
        )
        copy.start()
        self.pending.append(copy)
        return t

    def wait(self, t, dst):
        pltpu.make_async_remote_copy(
            dst, dst, self.send.at[t], self.recv.at[t],
            device_id=self.place.nb["y"], device_id_type=MESH,
        ).wait_recv()

    def drain(self):
        for copy in self.pending:
            copy.wait_send()


PARTS = (("x", "z", 0), ("z", "x", 1))


def load_tiles(tiles_hbm, tiles, sem):
    copies = [
        pltpu.make_async_copy(
            tiles_hbm.at[pl.ds(i * SLOTS // 4, SLOTS // 4)],
            tiles.at[pl.ds(i * SLOTS // 4, SLOTS // 4)],
            sem.at[i],
        )
        for i in range(4)
    ]
    for copy in copies:
        copy.start()
    return copies


def kernel(
    inv, f_ref, tiles_hbm, w_ref, ct_ref,
    out_ref, gi_ref, gw_ref,
    g, tiles, acc, in1, sbuf, in2, bt, gwp,
    pbuf, in_h, in_f, in_e, sb, in_h1, in_f1, tb, sy, in_y,
    gx, gz, gb, gacc, send, recv, loc,
):
    me = Place()
    me.barrier(("x+", "x-", "x2", "z+", "z-", "z2", "y", "core", "yh"))
    sends = Sends(me, send, recv)
    y, yp = me.y, me.yp
    ys = (y, yp)

    def rows(blk, lo, n):
        return g.at[blk, pl.ds(lo, n)]

    def push(where, blk, lo, n, mine=False):
        src = f_ref.at[pl.ds(lo, n)] if mine else rows(blk, lo, n)
        return sends.to(where, src, rows(blk, lo, n))

    def arrive(t, blk, lo, n):
        sends.wait(t, rows(blk, lo, n))

    p1, p1f, p2, p2f, far2, far3 = {}, {}, {}, {}, {}, {}

    def start2(s, p, d, mine=False):
        blk = me.at(ys[s], p[0], d, 0)
        lo = p[2] * HALF
        down = push(p[1] + "-", blk, lo, HALF, mine)
        p2[s, p[2], d] = (push(p[1] + "+", blk, lo, HALF, mine) if s == 0 else None, down)

    def stage1(s, mine):
        for p in PARTS:
            blk = me.at(ys[s], p[0], 0, 0)
            lo = p[2] * HALF
            p1[s, p[2]] = (push(p[0] + "+", blk, lo, HALF, mine), push(p[0] + "-", blk, lo, HALF, mine))
        for p in PARTS:
            start2(s, p, 0, mine)

    def stage2(s):
        for p in PARTS:
            lo = p[2] * HALF
            t = p1[s, p[2]]
            at = functools.partial(me.at, ys[s], p[0])
            arrive(t[0], at(-1, 0), lo, HALF)
            f0 = push(p[0] + "+", at(-1, 0), lo, QUARTER)
            start2(s, p, -1)
            arrive(t[1], at(1, 0), lo, HALF)
            f1 = push(p[0] + "-", at(1, 0), lo + QUARTER, QUARTER)
            start2(s, p, 1)
            p1f[s, p[2]] = (f0, f1)

    def stage3(s):
        for p in PARTS:
            lo = p[2] * HALF
            f0, f1 = p1f[s, p[2]]
            arrive(f0, me.at(ys[s], p[0], 2, 0), lo, QUARTER)
            arrive(f1, me.at(ys[s], p[0], 2, 0), lo + QUARTER, QUARTER)
            start2(s, p, 2)

    def stage4(d):
        for p in PARTS:
            lo = p[2] * HALF
            t = p2[0, p[2], d]
            at = functools.partial(me.at, y, p[0])
            arrive(t[0], at(d, -1), lo, HALF)
            far2[p[2], d] = push("y", at(d, -1), lo, HALF)
            f0 = push(p[1] + "+", at(d, -1), lo, QUARTER)
            arrive(t[1], at(d, 1), lo, HALF)
            p2f[p[2], d] = (f0, push(p[1] + "-", at(d, 1), lo + QUARTER, QUARTER))

    def stage5(d):
        for p in PARTS:
            lo = p[2] * HALF
            blk = me.at(y, p[0], d, 2)
            arrive(p2f[p[2], d][0], blk, lo, QUARTER)
            arrive(p2f[p[2], d][1], blk, lo + QUARTER, QUARTER)

    def stage6(d):
        for p in PARTS:
            blk = me.at(yp, p[0], d, -1)
            arrive(far2[p[2], d], blk, p[2] * HALF, HALF)
            far3[p[2], d] = push(p[1] + "+", blk, p[2] * HALF, HALF)

    def stage7(d):
        for p in PARTS:
            arrive(p2[1, p[2], d][1], me.at(yp, p[0], d, 1), p[2] * HALF, HALF)

    def stage8(d):
        for p in PARTS:
            arrive(far3[p[2], d], me.at(yp, p[0], d, 2), p[2] * HALF, HALF)

    def product(half, s, panels):
        blks = [(me.at(ys[s], p[0], d, e), p[2]) for d, e in panels for p in PARTS]
        lhs = []
        for blk, k in blks:
            for v in range(2):
                base = blk * 64 + half * 32 + k * 2 + v
                lhs.append(jnp.concatenate([tiles[inv[base + h * 4]] for h in range(8)], axis=0))
        lhs = jnp.concatenate(lhs, axis=1)
        rhs = jnp.concatenate([g[blk, pl.ds(k * HALF, HALF), :] for blk, k in blks], axis=0)
        return jnp.dot(lhs, rhs, preferred_element_type=f32)

    def compute(s, *panels, first=False):
        @pl.loop(0, 2)
        def _(half):
            if first:
                acc[half] = product(half, s, panels)
            else:
                acc[half] += product(half, s, panels)

    stage1(0, True)
    to_y = [push("y", me.b, i * HALF, HALF, True) for i in range(2)]
    own = pltpu.make_async_copy(f_ref, g.at[me.b], loc.at[4])
    own.start()
    loads = load_tiles(tiles_hbm, tiles, loc)
    tiles[SLOTS] = jnp.zeros((BS, BS), bf16)
    stage2(0)
    own.wait()
    for copy in loads:
        copy.wait()
    compute(0, (0, 0), (-1, 0), first=True)
    stage4(0)
    twin = me.blk(yp, me.c["z"], me.c["x"])
    for i in range(2):
        arrive(to_y[i], twin, i * HALF, HALF)
    stage1(1, False)
    stage3(0)
    compute(0, (0, -1), (0, 1))
    compute(0, (1, 0), (2, 0))
    stage4(-1)
    compute(0, (-1, -1), (-1, 1))
    stage4(1)
    stage6(0)
    compute(0, (1, -1), (1, 1))
    stage2(1)
    stage5(0)
    compute(1, (0, 0), (-1, 0))
    stage6(-1)
    stage4(2)
    stage3(1)
    stage5(-1)
    compute(0, (2, -1), (2, 1))
    stage6(1)
    compute(0, (0, 2), (-1, 2))
    compute(1, (1, 0), (2, 0))
    stage5(1)
    stage6(2)
    stage5(2)
    compute(0, (1, 2), (2, 2))
    compute(1, (0, -1), (-1, -1))
    compute(1, (1, -1), (2, -1))
    for d in (0, -1):
        stage7(d)
    compute(1, (0, 1), (-1, 1))
    for d in (1, 2):
        stage7(d)
    compute(1, (1, 1), (2, 1))
    for d in (0, -1):
        stage8(d)
    compute(1, (0, 2), (-1, 2))
    for d in (1, 2):
        stage8(d)

    far = 1 - me.yh
    other = 1 - me.core

    def last(half):
        acc[half] += product(half, 1, ((1, 2), (2, 2)))

    theirs = pl.ds(other * PANEL, PANEL)
    last(far)
    t_far = sends.to("core", acc.at[far, theirs], in1.at[far])
    last(me.yh)
    t_near = sends.to("core", acc.at[me.yh, theirs], in1.at[me.yh])
    sends.wait(t_far, in1.at[far])
    t_yh = []
    for i in range(2):
        part = pl.ds(i * HALF, HALF)
        mine = acc[far, pl.ds(me.core * PANEL + i * HALF, HALF), :]
        sbuf[i] = (mine + in1[far, part, :]).astype(bf16)
        t_yh.append(sends.to("yh", sbuf.at[i], in2.at[i]))
    sends.wait(t_near, in1.at[me.yh])
    t_bt = []
    for i in range(2):
        part = pl.ds(i * HALF, HALF)
        sends.wait(t_yh[i], in2.at[i])
        mine = acc[me.yh, pl.ds(me.core * PANEL + i * HALF, HALF), :]
        agg = (mine + in1[me.yh, part, :] + in2[i].astype(f32)).astype(bf16)
        linear = jnp.dot(agg, w_ref[...], preferred_element_type=f32)
        sigma = 1.0 / (1.0 + jnp.exp(-linear))
        gl = (ct_ref[part, :].astype(f32) * sigma * (1.0 + linear * (1.0 - sigma))).astype(bf16)
        back = lax.dot_general(w_ref[...], gl, (((1,), (1,)), ((), ())), preferred_element_type=f32)
        mine = bt.at[me.r * 2 + i]
        bt[me.r * 2 + i] = back.astype(bf16)
        t_bt.append((sends.to("yh", mine, mine), sends.to("core", mine, mine)))
        out_ref[part, :] = (linear * sigma).astype(bf16)
        local_gw = lax.dot_general(agg, gl, (((0,), (0,)), ((), ())), preferred_element_type=f32)
        if i == 0:
            gwp[...] = local_gw
        else:
            gwp[...] += local_gw

    cx, cz = me.c["x"], me.c["z"]

    def piece(axis_x, n, ref):
        return ref.at[pl.ds(axis_x * n, n)]

    hops = ((1, "+"), (2, "2"), (3, "-"))
    gstate = {}

    def gw_step(n):
        if n == 0:
            gstate["x"] = [
                sends.to("x" + name, piece(me.up("x", step), 64, gwp), gx.at[i])
                for i, (step, name) in enumerate(hops)
            ]
        elif n == 1:
            total = gwp[pl.ds(cx * 64, 64), :]
            for i in range(3):
                sends.wait(gstate["x"][i], gx.at[i])
                total = total + gx[i]
            gacc[0] = total
            gstate["z"] = [
                sends.to("z" + name, gacc.at[0, pl.ds(me.up("z", step) * 16, 16)], gz.at[i])
                for i, (step, name) in enumerate(hops)
            ]
        elif n == 2:
            total = gacc[0, pl.ds(cz * 16, 16), :]
            for i in range(3):
                sends.wait(gstate["z"][i], gz.at[i])
                total = total + gz[i]
            gb[0] = total
            gstate["b"] = sends.to("core", gb.at[0], gb.at[3])
        elif n in (3, 4):
            k = n - 3
            sends.wait(gstate["b"], gb.at[k + 3])
            gb[k + 1] = gb[k] + gb[k + 3]
            gstate["b"] = sends.to(("yh", "y")[k], gb.at[k + 1], gb.at[k + 4])
        elif n == 5:
            sends.wait(gstate["b"], gb.at[5])
            gacc[1, pl.ds(cz * 16, 16), :] = (gb[2] + gb[5]) * f32(1.0 / math.sqrt(65536))
            mine = gacc.at[1, pl.ds(cz * 16, 16)]
            gstate["az"] = [sends.to("z" + name, mine, mine) for _, name in hops]
        elif n == 6:
            for i, (step, _) in enumerate(hops):
                sends.wait(gstate["az"][i], gacc.at[1, pl.ds(me.up("z", -step) * 16, 16)])
            gw_ref[pl.ds(cx * 64, 64), :] = gacc[1]
            mine = piece(cx, 64, gw_ref)
            gstate["ax"] = [sends.to("x" + name, mine, mine) for _, name in hops]
        else:
            for i, (step, _) in enumerate(hops):
                sends.wait(gstate["ax"][i], piece(me.up("x", -step), 64, gw_ref))

    there = far * 2 + me.core
    b_fwd = []
    for i in range(2):
        src = bt.at[there * 2 + i]
        sends.wait(t_bt[i][0], src)
        b_fwd.append(sends.to("core", src, src))
    for i in range(2):
        sends.wait(t_bt[i][1], bt.at[(me.yh * 2 + other) * 2 + i])
        sends.wait(b_fwd[i], bt.at[(far * 2 + other) * 2 + i])

    D = (2, -1, 1, 0)
    lo, hi = pl.ds(0, QUARTER), pl.ds(QUARTER, QUARTER)
    halves, fulls, halves1, fulls1, to_e = {}, {}, {}, {}, {}

    def slot(s, d, p):
        return (s * 4 + D.index(d)) * 2 + p[2]

    def wide(ref, *at):
        return ref[at].astype(f32)

    def spread(s, d, p):
        q = slot(s, d, p)

        def pair(*es):
            cols = []
            for e in es:
                base = me.at(ys[s], p[0], d, e) * 64 + p[2] * 2
                for v in range(2):
                    cols.append(jnp.concatenate([tiles[inv[base + v + h * 4]] for h in range(16)], axis=0))
            rhs = jnp.concatenate(cols, axis=1)
            lhs = jnp.concatenate([bt[i] for i in range(8)], axis=1)
            both = jnp.dot(lhs, rhs, preferred_element_type=f32).astype(bf16)
            for i, e in enumerate(es):
                pbuf[q, e] = both[:, i * HALF:(i + 1) * HALF]

        u = slot(0, d, p)
        if s == 1:
            pair(1, 3)
            fulls[q] = (
                sends.to(p[1] + "+", pbuf.at[q, 1], in_f.at[q, 0]),
                sends.to(p[1] + "-", pbuf.at[q, 3], in_f.at[q, 1]),
            )
            pair(2, 0)
            to_e[u] = sends.to("y", pbuf.at[q, 2], in_e.at[u])
        else:
            pair(2, 1)
            sends.wait(to_e[u], in_e.at[u])
            pbuf[q, 2] = (wide(pbuf, q, 2) + wide(in_e, u)).astype(bf16)
            halves[q] = (
                sends.to(p[1] + "+", pbuf.at[q, 2, lo], in_h.at[q, 0]),
                sends.to(p[1] + "-", pbuf.at[q, 2, hi], in_h.at[q, 1]),
            )
            pair(3, 0)

    def second(s, d, p):
        if s == 1:
            return
        q = slot(s, d, p)
        t = halves[q]
        sends.wait(t[0], in_h.at[q, 0])
        pbuf[q, 1, lo, :] = (pbuf[q, 1, lo, :].astype(f32) + wide(in_h, q, 0)).astype(bf16)
        up = sends.to(p[1] + "+", pbuf.at[q, 1], in_f.at[q, 0])
        sends.wait(t[1], in_h.at[q, 1])
        pbuf[q, 3, hi, :] = (pbuf[q, 3, hi, :].astype(f32) + wide(in_h, q, 1)).astype(bf16)
        down = sends.to(p[1] + "-", pbuf.at[q, 3], in_f.at[q, 1])
        fulls[q] = (up, down)

    def third(s, d, p):
        q = slot(s, d, p)
        t = fulls[q]
        u = s * 2 + p[2]
        sends.wait(t[0], in_f.at[q, 0])
        sends.wait(t[1], in_f.at[q, 1])
        total = wide(pbuf, q, 0) + wide(in_f, q, 0) + wide(in_f, q, 1)
        if d == 2:
            sb[u, 0] = total.astype(bf16)
            halves1[u] = (
                sends.to(p[0] + "+", sb.at[u, 0, lo], in_h1.at[u, 0]),
                sends.to(p[0] + "-", sb.at[u, 0, hi], in_h1.at[u, 1]),
            )
        elif d == 1:
            sb[u, 1] = total.astype(bf16)
            sends.wait(halves1[u][0], in_h1.at[u, 0])
            sb[u, 1, lo, :] = (total[:QUARTER] + wide(in_h1, u, 0)).astype(bf16)
            fulls1[u, 0] = sends.to(p[0] + "+", sb.at[u, 1], in_f1.at[u, 0])
        elif d == -1:
            sb[u, 2] = total.astype(bf16)
            sends.wait(halves1[u][1], in_h1.at[u, 1])
            sb[u, 2, hi, :] = (total[QUARTER:] + wide(in_h1, u, 1)).astype(bf16)
            fulls1[u, 1] = sends.to(p[0] + "-", sb.at[u, 2], in_f1.at[u, 1])
        else:
            tb[p[2]] = total

    home = {}

    def fourth(s, p):
        u = s * 2 + p[2]
        for i in range(2):
            sends.wait(fulls1[u, i], in_f1.at[u, i])
        total = tb[p[2]] + wide(in_f1, u, 0) + wide(in_f1, u, 1)
        if s == 1:
            sy[p[2]] = total.astype(bf16)
            home[p[2]] = sends.to("y", sy.at[p[2]], in_y.at[p[2]])
        else:
            sends.wait(home[p[2]], in_y.at[p[2]])
            total = total + wide(in_y, p[2])
            gi_ref[pl.ds(p[2] * HALF, HALF), :] = total.T

    steps = [(s, d) for s in (1, 0) for d in D]
    n = len(steps)

    def both(fn, step):
        for p in PARTS:
            fn(*step, p)

    for i in range(n + 2):
        if i < n:
            both(spread, steps[i])
        if 1 <= i <= n:
            both(second, steps[i - 1])
        if i >= 2:
            both(third, steps[i - 2])
            if i - 2 == 3:
                for p in PARTS:
                    fourth(1, p)
        if i <= 7:
            gw_step(i)
    for p in PARTS:
        fourth(0, p)
    sends.drain()
    assert sends.count <= SENDS


def copy_kernel(*refs):
    k = len(refs) // 2
    for i in range(k):
        refs[k + i][...] = refs[i][...]


def inverse(bands, cols, counts):
    slots = jnp.arange(CAP, dtype=jnp.int32)
    where = jnp.where(slots[None] < counts[:, None], bands * 4 + cols, -1)
    ids = jnp.arange(SLOTS, dtype=jnp.int32).reshape(PANELS, CAP) - SLOTS
    hit = where[:, None, :] == jnp.arange(64, dtype=jnp.int32)[None, :, None]
    return (jnp.sum(jnp.where(hit, ids[:, None, :], 0), axis=2) + SLOTS).reshape(-1)


def local(features, tiles, bands, cols, counts, weight, cotangent):
    inv = inverse(bands[0, 0], cols[0, 0], counts[0, 0])
    tiles = tiles.reshape(SLOTS, BS, BS)
    vmem = pl.BlockSpec(memory_space=pltpu.VMEM)
    hbm = pl.BlockSpec(memory_space=pl.ANY)
    smem = pl.BlockSpec(memory_space=pltpu.SMEM)
    dma = pltpu.SemaphoreType.DMA
    results = (
        jax.ShapeDtypeStruct((PANEL, F), bf16),
        jax.ShapeDtypeStruct((PANEL, F), f32),
        jax.ShapeDtypeStruct((F, F), f32),
    )
    results = pl.pallas_call(
        kernel,
        out_shape=results,
        in_specs=[smem, vmem, hbm, vmem, vmem],
        out_specs=(vmem, vmem, vmem),
        scratch_shapes=[
            pltpu.VMEM((PANELS, PANEL, F), bf16),
            pltpu.VMEM((SLOTS + 1, BS, BS), bf16),
            pltpu.VMEM((2, 2 * PANEL, F), f32),
            pltpu.VMEM((2, PANEL, F), f32),
            pltpu.VMEM((2, HALF, F), bf16),
            pltpu.VMEM((2, HALF, F), bf16),
            pltpu.VMEM((8, F, HALF), bf16),
            pltpu.VMEM((F, F), f32),
            pltpu.VMEM((16, 4, F, HALF), bf16),
            pltpu.VMEM((8, 2, QUARTER, HALF), bf16),
            pltpu.VMEM((16, 2, F, HALF), bf16),
            pltpu.VMEM((8, F, HALF), bf16),
            pltpu.VMEM((4, 3, F, HALF), bf16),
            pltpu.VMEM((4, 2, QUARTER, HALF), bf16),
            pltpu.VMEM((4, 2, F, HALF), bf16),
            pltpu.VMEM((2, F, HALF), f32),
            pltpu.VMEM((2, F, HALF), bf16),
            pltpu.VMEM((2, F, HALF), bf16),
            pltpu.VMEM((3, 64, F), f32),
            pltpu.VMEM((3, 16, F), f32),
            pltpu.VMEM((6, 16, F), f32),
            pltpu.VMEM((2, 64, F), f32),
            dma((SENDS,)), dma((SENDS,)), dma((5,)),
        ],
        compiler_params=pltpu.CompilerParams(
            collective_id=0, has_side_effects=True, vmem_limit_bytes=58 * 2**20
        ),
        name="graph_layer",
    )(inv, features, tiles, weight, cotangent)
    output, grad_input, grad_weight = pl.pallas_call(
        copy_kernel,
        out_shape=tuple(jax.ShapeDtypeStruct(x.shape, x.dtype) for x in results),
        in_specs=[vmem] * 3,
        out_specs=(vmem,) * 3,
        name="results",
    )(*results)
    return output, grad_weight, grad_input


def solution(mesh):
    placed = (
        P(("blk", "rep"), None),
        P("blk", "rep", None, None, None, None),
        P("blk", "rep", None, None),
        P("blk", "rep", None, None),
        P("blk", "rep", None),
        P(),
        P(("blk", "rep"), None),
    )
    return jax.shard_map(
        local,
        mesh=mesh,
        in_specs=placed,
        out_specs=(P(("blk", "rep"), None), P(), P(("blk", "rep"), None)),
        check_vma=False,
    )
```

```python
import functools
import math

import jax
import jax.numpy as jnp
from jax import lax
from jax.experimental import pallas as pl
from jax.experimental.pallas import tpu as pltpu
from jax.sharding import PartitionSpec as P

MESH = pl.DeviceIdType.MESH
F = 256
BS = 128
CAP = 12
PANELS = 32
PANEL = 512
HALF = 256
QUARTER = 128
SLOTS = PANELS * CAP
SENDS = 200
bf16 = jnp.bfloat16
f32 = jnp.float32


class Place:
    def __init__(self):
        b = lax.axis_index("blk")
        r = lax.axis_index("rep")
        self.b, self.r = b, r
        self.c = {"x": lax.rem(b, 4), "z": lax.rem(b // 4, 4)}
        self.y = b // 16
        self.yp = 1 - self.y
        self.core = lax.rem(r, 2)
        self.yh = r // 2
        self.nb = {"y": {"blk": self.blk(self.yp, self.c["z"], self.c["x"])}}
        for axis in ("x", "z"):
            for name, step in (("+", 1), ("-", -1), ("2", 2)):
                self.nb[axis + name] = {"blk": self.at(self.y, axis, step, 0)}
        self.nb["core"] = {"rep": self.yh * 2 + 1 - self.core}
        self.nb["yh"] = {"rep": (1 - self.yh) * 2 + self.core}

    def blk(self, y, z, x):
        return y * 16 + z * 4 + x

    def up(self, axis, step):
        return lax.rem(self.c[axis] + step + 4, 4)

    def at(self, y, first, d, e):
        if first == "x":
            return self.blk(y, self.up("z", e), self.up("x", d))
        return self.blk(y, self.up("z", d), self.up("x", e))

    def on_second(self, y, first, d, e):
        if first == "x":
            return self.blk(y, e, self.up("x", d))
        return self.blk(y, self.up("z", d), e)

    def barrier(self, names):
        sem = pltpu.get_barrier_semaphore()
        for name in names:
            pl.semaphore_signal(sem, inc=1, device_id=self.nb[name], device_id_type=MESH)
        pl.semaphore_wait(sem, len(names))


class Sends:
    def __init__(self, place, send, recv):
        self.place, self.send, self.recv = place, send, recv
        self.count = 0
        self.pending = []

    def to(self, where, src, dst):
        t = self.count
        self.count += 1
        copy = pltpu.make_async_remote_copy(
            src, dst, self.send.at[t], self.recv.at[t],
            device_id=self.place.nb[where], device_id_type=MESH,
        )
        copy.start()
        self.pending.append(copy)
        return t

    def wait(self, t, dst):
        pltpu.make_async_remote_copy(
            dst, dst, self.send.at[t], self.recv.at[t],
            device_id=self.place.nb["y"], device_id_type=MESH,
        ).wait_recv()

    def drain(self):
        for copy in self.pending:
            copy.wait_send()


PARTS = (("x", "z", 0), ("z", "x", 1))


def load_tiles(tiles_hbm, tiles, sem):
    copies = [
        pltpu.make_async_copy(
            tiles_hbm.at[pl.ds(i * SLOTS // 4, SLOTS // 4)],
            tiles.at[pl.ds(i * SLOTS // 4, SLOTS // 4)],
            sem.at[i],
        )
        for i in range(4)
    ]
    for copy in copies:
        copy.start()
    return copies


def kernel(
    inv, f_ref, tiles_hbm, w_ref, ct_ref,
    out_ref, gi_ref, gw_ref,
    g, tiles, acc, in1, sbuf, in2, bt, gwp,
    pbuf, in_h, in_f, in_e, sb, in_h1, in_f1, tb, sy, in_y,
    gc, ga, gy, gq, gx, gz, gb, gr, go, send, recv, loc,
):
    me = Place()
    me.barrier(("x+", "x-", "x2", "z+", "z-", "z2", "y", "core", "yh"))
    sends = Sends(me, send, recv)
    y, yp = me.y, me.yp
    ys = (y, yp)

    def rows(blk, lo, n):
        return g.at[blk, pl.ds(lo, n)]

    def push(where, blk, lo, n, mine=False):
        src = f_ref.at[pl.ds(lo, n)] if mine else rows(blk, lo, n)
        return sends.to(where, src, rows(blk, lo, n))

    def arrive(t, blk, lo, n):
        sends.wait(t, rows(blk, lo, n))

    p1, p1f, p2, p2f, far2, far3 = {}, {}, {}, {}, {}, {}

    def start2(s, p, d, mine=False):
        blk = me.at(ys[s], p[0], d, 0)
        lo = p[2] * HALF
        down = push(p[1] + "-", blk, lo, HALF, mine)
        p2[s, p[2], d] = (push(p[1] + "+", blk, lo, HALF, mine) if s == 0 else None, down)

    def stage1(s, mine):
        for p in PARTS:
            blk = me.at(ys[s], p[0], 0, 0)
            lo = p[2] * HALF
            p1[s, p[2]] = (push(p[0] + "+", blk, lo, HALF, mine), push(p[0] + "-", blk, lo, HALF, mine))
        for p in PARTS:
            start2(s, p, 0, mine)

    def stage2(s):
        for p in PARTS:
            lo = p[2] * HALF
            t = p1[s, p[2]]
            at = functools.partial(me.at, ys[s], p[0])
            arrive(t[0], at(-1, 0), lo, HALF)
            f0 = push(p[0] + "+", at(-1, 0), lo, QUARTER)
            start2(s, p, -1)
            arrive(t[1], at(1, 0), lo, HALF)
            f1 = push(p[0] + "-", at(1, 0), lo + QUARTER, QUARTER)
            start2(s, p, 1)
            p1f[s, p[2]] = (f0, f1)

    def stage3(s):
        for p in PARTS:
            lo = p[2] * HALF
            f0, f1 = p1f[s, p[2]]
            arrive(f0, me.at(ys[s], p[0], 2, 0), lo, QUARTER)
            arrive(f1, me.at(ys[s], p[0], 2, 0), lo + QUARTER, QUARTER)
            start2(s, p, 2)

    def stage4(d):
        for p in PARTS:
            lo = p[2] * HALF
            t = p2[0, p[2], d]
            at = functools.partial(me.at, y, p[0])
            arrive(t[0], at(d, -1), lo, HALF)
            far2[p[2], d] = push("y", at(d, -1), lo, HALF)
            f0 = push(p[1] + "+", at(d, -1), lo, QUARTER)
            arrive(t[1], at(d, 1), lo, HALF)
            p2f[p[2], d] = (f0, push(p[1] + "-", at(d, 1), lo + QUARTER, QUARTER))

    def stage5(d):
        for p in PARTS:
            lo = p[2] * HALF
            blk = me.at(y, p[0], d, 2)
            arrive(p2f[p[2], d][0], blk, lo, QUARTER)
            arrive(p2f[p[2], d][1], blk, lo + QUARTER, QUARTER)

    def stage6(d):
        for p in PARTS:
            blk = me.at(yp, p[0], d, -1)
            arrive(far2[p[2], d], blk, p[2] * HALF, HALF)
            far3[p[2], d] = push(p[1] + "+", blk, p[2] * HALF, HALF)

    def stage7(d):
        for p in PARTS:
            arrive(p2[1, p[2], d][1], me.at(yp, p[0], d, 1), p[2] * HALF, HALF)

    def stage8(d):
        for p in PARTS:
            arrive(far3[p[2], d], me.at(yp, p[0], d, 2), p[2] * HALF, HALF)

    def product(half, s, panels):
        blks = [(me.at(ys[s], p[0], d, e), p[2]) for d, e in panels for p in PARTS]
        lhs = []
        for blk, k in blks:
            for v in range(2):
                base = half * 32 + k * 2 + v
                lhs.append(jnp.concatenate([tiles[inv[blk, base + h * 4]] for h in range(8)], axis=0))
        lhs = jnp.concatenate(lhs, axis=1)
        rhs = jnp.concatenate([g[blk, pl.ds(k * HALF, HALF), :] for blk, k in blks], axis=0)
        return jnp.dot(lhs, rhs, preferred_element_type=f32)

    def compute(s, *panels, first=False):
        @pl.loop(0, 2)
        def _(half):
            if first:
                acc[half] = product(half, s, panels)
            else:
                acc[half] += product(half, s, panels)

    far = 1 - me.yh
    other = 1 - me.core
    later = []

    def first_far(s, *panels):
        acc[far] += product(far, s, panels)
        later.append((s, panels))

    def catch_up(n):
        for s, panels in later[:n]:
            acc[me.yh] += product(me.yh, s, panels)
        del later[:n]

    stage1(0, True)
    to_y = [push("y", me.b, i * HALF, HALF, True) for i in range(2)]
    own = pltpu.make_async_copy(f_ref, g.at[me.b], loc.at[4])
    own.start()
    loads = load_tiles(tiles_hbm, tiles, loc)
    tiles[SLOTS] = jnp.zeros((BS, BS), bf16)
    stage2(0)
    own.wait()
    for copy in loads:
        copy.wait()
    compute(0, (0, 0), (-1, 0), first=True)
    stage4(0)
    twin = me.blk(yp, me.c["z"], me.c["x"])
    for i in range(2):
        arrive(to_y[i], twin, i * HALF, HALF)
    stage1(1, False)
    stage3(0)
    compute(0, (0, -1), (0, 1))
    compute(0, (1, 0), (2, 0))
    stage4(-1)
    compute(0, (-1, -1), (-1, 1))
    stage4(1)
    stage6(0)
    compute(0, (1, -1), (1, 1))
    stage2(1)
    stage5(0)
    compute(1, (0, 0), (-1, 0))
    stage6(-1)
    stage4(2)
    stage3(1)
    stage5(-1)
    compute(0, (2, -1), (2, 1))
    stage6(1)
    compute(0, (0, 2), (-1, 2))
    compute(1, (1, 0), (2, 0))
    stage5(1)
    stage6(2)
    stage5(2)
    first_far(0, (1, 2), (2, 2))
    first_far(1, (0, -1), (-1, -1))
    first_far(1, (1, -1), (2, -1))
    for d in (0, -1):
        stage7(d)
    first_far(1, (0, 1), (-1, 1))
    for d in (1, 2):
        stage7(d)
    first_far(1, (1, 1), (2, 1))
    for d in (0, -1):
        stage8(d)
    first_far(1, (0, 2), (-1, 2))
    for d in (1, 2):
        stage8(d)
    first_far(1, (1, 2), (2, 2))

    theirs = pl.ds(other * PANEL, PANEL)
    t_far = sends.to("core", acc.at[far, theirs], in1.at[far])
    catch_up(3)
    sends.wait(t_far, in1.at[far])
    t_yh = []
    for i in range(2):
        part = pl.ds(i * HALF, HALF)
        mine = acc[far, pl.ds(me.core * PANEL + i * HALF, HALF), :]
        sbuf[i] = (mine + in1[far, part, :]).astype(bf16)
        t_yh.append(sends.to("yh", sbuf.at[i], in2.at[i]))
    catch_up(len(later))
    t_near = sends.to("core", acc.at[me.yh, theirs], in1.at[me.yh])
    sends.wait(t_near, in1.at[me.yh])
    t_bt = []
    for i in range(2):
        part = pl.ds(i * HALF, HALF)
        sends.wait(t_yh[i], in2.at[i])
        mine = acc[me.yh, pl.ds(me.core * PANEL + i * HALF, HALF), :]
        agg = (mine + in1[me.yh, part, :] + in2[i].astype(f32)).astype(bf16)
        linear = jnp.dot(agg, w_ref[...], preferred_element_type=f32)
        sigma = 1.0 / (1.0 + jnp.exp(-linear))
        gl = (ct_ref[part, :].astype(f32) * sigma * (1.0 + linear * (1.0 - sigma))).astype(bf16)
        back = lax.dot_general(w_ref[...], gl, (((1,), (1,)), ((), ())), preferred_element_type=f32)
        mine = bt.at[me.r * 2 + i]
        bt[me.r * 2 + i] = back.astype(bf16)
        t_bt.append((sends.to("yh", mine, mine), sends.to("core", mine, mine)))
        out_ref[part, :] = (linear * sigma).astype(bf16)
        local_gw = lax.dot_general(agg, gl, (((0,), (0,)), ((), ())), preferred_element_type=f32)
        if i == 0:
            gwp[...] = local_gw
        else:
            gwp[...] += local_gw

    cx, cz = me.c["x"], me.c["z"]
    hops = ((1, "+"), (2, "2"), (3, "-"))
    gstate = {}

    def gw_step(n):
        t = gstate.get("t")
        if n == 0:
            gstate["t"] = sends.to("core", gwp.at[pl.ds(other * 128, 128)], gc)
        elif n == 1:
            sends.wait(t, gc)
            ga[...] = gwp[pl.ds(me.core * 128, 128), :] + gc[...]
            gstate["t"] = sends.to("y", ga.at[pl.ds(yp * 64, 64)], gy)
        elif n == 2:
            sends.wait(t, gy)
            gq[...] = ga[pl.ds(y * 64, 64), :] + gy[...]
            gstate["t"] = [
                sends.to("x" + name, gq.at[pl.ds(me.up("x", step) * 16, 16)], gx.at[i])
                for i, (step, name) in enumerate(hops)
            ]
        elif n == 3:
            total = gq[pl.ds(cx * 16, 16), :]
            for i in range(3):
                sends.wait(t[i], gx.at[i])
                total = total + gx[i]
            gz[cz] = total
            gstate["t"] = [sends.to("z" + name, gz.at[cz], gz.at[cz]) for _, name in hops]
        elif n == 4:
            for i, (step, _) in enumerate(hops):
                sends.wait(t[i], gz.at[me.up("z", -step)])
            gb[0] = (gz[0] + gz[1]) + (gz[2] + gz[3])
            gstate["t"] = sends.to("yh", gb.at[0], gb.at[1])
        elif n == 5:
            sends.wait(t, gb.at[1])
            gr[pl.ds(cx * 16, 16), :] = (gb[0] + gb[1]) * f32(1.0 / math.sqrt(65536))
            mine = gr.at[pl.ds(cx * 16, 16)]
            gstate["t"] = [sends.to("x" + name, mine, mine) for _, name in hops]
        elif n == 6:
            for i, (step, _) in enumerate(hops):
                sends.wait(t[i], gr.at[pl.ds(me.up("x", -step) * 16, 16)])
            go[pl.ds(y * 64, 64), :] = gr[...]
            mine = go.at[pl.ds(y * 64, 64)]
            gstate["t"] = sends.to("y", mine, mine)
        elif n == 7:
            sends.wait(t, go.at[pl.ds(yp * 64, 64)])
            gw_ref[pl.ds(me.core * 128, 128), :] = go[...]
            mine = gw_ref.at[pl.ds(me.core * 128, 128)]
            gstate["t"] = sends.to("core", mine, mine)
        elif n == 8:
            sends.wait(t, gw_ref.at[pl.ds(other * 128, 128)])

    there = far * 2 + me.core
    b_fwd = []
    for i in range(2):
        src = bt.at[there * 2 + i]
        sends.wait(t_bt[i][0], src)
        b_fwd.append(sends.to("core", src, src))
    for i in range(2):
        sends.wait(t_bt[i][1], bt.at[(me.yh * 2 + other) * 2 + i])
        sends.wait(b_fwd[i], bt.at[(far * 2 + other) * 2 + i])

    D = (2, -1, 1, 0)
    lo, hi = pl.ds(0, QUARTER), pl.ds(QUARTER, QUARTER)
    halves, fulls, halves1, fulls1, to_e = {}, {}, {}, {}, {}

    def slot(s, d, p):
        return (s * 4 + D.index(d)) * 2 + p[2]

    def wide(ref, *at):
        return ref[at].astype(f32)

    def spread(s, d, p):
        q = slot(s, d, p)

        def pair(*es):
            cols = []
            for e in es:
                blk = me.at(ys[s], p[0], d, e)
                for v in range(2):
                    cols.append(jnp.concatenate([tiles[inv[blk, p[2] * 2 + v + h * 4]] for h in range(16)], axis=0))
            rhs = jnp.concatenate(cols, axis=1)
            lhs = jnp.concatenate([bt[i] for i in range(8)], axis=1)
            both = jnp.dot(lhs, rhs, preferred_element_type=f32).astype(bf16)
            for i, e in enumerate(es):
                pbuf[q, e] = both[:, i * HALF:(i + 1) * HALF]

        u = slot(0, d, p)
        if s == 1:
            pair(1, 3)
            fulls[q] = (
                sends.to(p[1] + "+", pbuf.at[q, 1], in_f.at[q, 0]),
                sends.to(p[1] + "-", pbuf.at[q, 3], in_f.at[q, 1]),
            )
            pair(2, 0)
            to_e[u] = sends.to("y", pbuf.at[q, 2], in_e.at[u])
        else:
            pair(2, 1)
            sends.wait(to_e[u], in_e.at[u])
            pbuf[q, 2] = (wide(pbuf, q, 2) + wide(in_e, u)).astype(bf16)
            halves[q] = (
                sends.to(p[1] + "+", pbuf.at[q, 2, lo], in_h.at[q, 0]),
                sends.to(p[1] + "-", pbuf.at[q, 2, hi], in_h.at[q, 1]),
            )
            pair(3, 0)

    def second(s, d, p):
        if s == 1:
            return
        q = slot(s, d, p)
        t = halves[q]
        sends.wait(t[0], in_h.at[q, 0])
        pbuf[q, 1, lo, :] = (pbuf[q, 1, lo, :].astype(f32) + wide(in_h, q, 0)).astype(bf16)
        up = sends.to(p[1] + "+", pbuf.at[q, 1], in_f.at[q, 0])
        sends.wait(t[1], in_h.at[q, 1])
        pbuf[q, 3, hi, :] = (pbuf[q, 3, hi, :].astype(f32) + wide(in_h, q, 1)).astype(bf16)
        down = sends.to(p[1] + "-", pbuf.at[q, 3], in_f.at[q, 1])
        fulls[q] = (up, down)

    def third(s, d, p):
        q = slot(s, d, p)
        t = fulls[q]
        u = s * 2 + p[2]
        sends.wait(t[0], in_f.at[q, 0])
        sends.wait(t[1], in_f.at[q, 1])
        total = wide(pbuf, q, 0) + wide(in_f, q, 0) + wide(in_f, q, 1)
        if d == 2:
            sb[u, 0] = total.astype(bf16)
            halves1[u] = (
                sends.to(p[0] + "+", sb.at[u, 0, lo], in_h1.at[u, 0]),
                sends.to(p[0] + "-", sb.at[u, 0, hi], in_h1.at[u, 1]),
            )
        elif d == 1:
            sb[u, 1] = total.astype(bf16)
            sends.wait(halves1[u][0], in_h1.at[u, 0])
            sb[u, 1, lo, :] = (total[:QUARTER] + wide(in_h1, u, 0)).astype(bf16)
            fulls1[u, 0] = sends.to(p[0] + "+", sb.at[u, 1], in_f1.at[u, 0])
        elif d == -1:
            sb[u, 2] = total.astype(bf16)
            sends.wait(halves1[u][1], in_h1.at[u, 1])
            sb[u, 2, hi, :] = (total[QUARTER:] + wide(in_h1, u, 1)).astype(bf16)
            fulls1[u, 1] = sends.to(p[0] + "-", sb.at[u, 2], in_f1.at[u, 1])
        else:
            tb[p[2]] = total

    home = {}

    def fourth(s, p):
        u = s * 2 + p[2]
        for i in range(2):
            sends.wait(fulls1[u, i], in_f1.at[u, i])
        total = tb[p[2]] + wide(in_f1, u, 0) + wide(in_f1, u, 1)
        if s == 1:
            sy[p[2]] = total.astype(bf16)
            home[p[2]] = sends.to("y", sy.at[p[2]], in_y.at[p[2]])
        else:
            sends.wait(home[p[2]], in_y.at[p[2]])
            total = total + wide(in_y, p[2])
            gi_ref[pl.ds(p[2] * HALF, HALF), :] = total.T

    steps = [(s, d) for s in (1, 0) for d in D]
    n = len(steps)

    def both(fn, step):
        for p in PARTS:
            fn(*step, p)

    for i in range(n + 2):
        if i < n:
            both(spread, steps[i])
        if 1 <= i <= n:
            both(second, steps[i - 1])
        if i >= 2:
            both(third, steps[i - 2])
            if i - 2 == 3:
                for p in PARTS:
                    fourth(1, p)
        gw_step(i)
    for p in PARTS:
        fourth(0, p)
    sends.drain()
    assert sends.count <= SENDS


def copy_kernel(*refs):
    k = len(refs) // 2
    for i in range(k):
        refs[k + i][...] = refs[i][...]


def inverse(bands, cols, counts):
    slots = jnp.arange(CAP, dtype=jnp.int32)
    where = jnp.where(slots[None] < counts[:, None], bands * 4 + cols, -1)
    ids = jnp.arange(SLOTS, dtype=jnp.int32).reshape(PANELS, CAP) - SLOTS
    hit = where[:, None, :] == jnp.arange(64, dtype=jnp.int32)[None, :, None]
    return jnp.sum(jnp.where(hit, ids[:, None, :], 0), axis=2) + SLOTS


def local(features, tiles, bands, cols, counts, weight, cotangent):
    inv = inverse(bands[0, 0], cols[0, 0], counts[0, 0])
    tiles = tiles.reshape(SLOTS, BS, BS)
    vmem = pl.BlockSpec(memory_space=pltpu.VMEM)
    hbm = pl.BlockSpec(memory_space=pl.ANY)
    smem = pl.BlockSpec(memory_space=pltpu.SMEM)
    dma = pltpu.SemaphoreType.DMA
    results = (
        jax.ShapeDtypeStruct((PANEL, F), bf16),
        jax.ShapeDtypeStruct((PANEL, F), f32),
        jax.ShapeDtypeStruct((F, F), f32),
    )
    results = pl.pallas_call(
        kernel,
        out_shape=results,
        in_specs=[smem, vmem, hbm, vmem, vmem],
        out_specs=(vmem, vmem, vmem),
        scratch_shapes=[
            pltpu.VMEM((PANELS, PANEL, F), bf16),
            pltpu.VMEM((SLOTS + 1, BS, BS), bf16),
            pltpu.VMEM((2, 2 * PANEL, F), f32),
            pltpu.VMEM((2, PANEL, F), f32),
            pltpu.VMEM((2, HALF, F), bf16),
            pltpu.VMEM((2, HALF, F), bf16),
            pltpu.VMEM((8, F, HALF), bf16),
            pltpu.VMEM((F, F), f32),
            pltpu.VMEM((16, 4, F, HALF), bf16),
            pltpu.VMEM((8, 2, QUARTER, HALF), bf16),
            pltpu.VMEM((16, 2, F, HALF), bf16),
            pltpu.VMEM((8, F, HALF), bf16),
            pltpu.VMEM((4, 3, F, HALF), bf16),
            pltpu.VMEM((4, 2, QUARTER, HALF), bf16),
            pltpu.VMEM((4, 2, F, HALF), bf16),
            pltpu.VMEM((2, F, HALF), f32),
            pltpu.VMEM((2, F, HALF), bf16),
            pltpu.VMEM((2, F, HALF), bf16),
            pltpu.VMEM((128, F), f32),
            pltpu.VMEM((128, F), f32),
            pltpu.VMEM((64, F), f32),
            pltpu.VMEM((64, F), f32),
            pltpu.VMEM((3, 16, F), f32),
            pltpu.VMEM((4, 16, F), f32),
            pltpu.VMEM((2, 16, F), f32),
            pltpu.VMEM((64, F), f32),
            pltpu.VMEM((128, F), f32),
            dma((SENDS,)), dma((SENDS,)), dma((5,)),
        ],
        compiler_params=pltpu.CompilerParams(
            collective_id=0, has_side_effects=True, vmem_limit_bytes=58 * 2**20
        ),
        name="graph_layer",
    )(inv, features, tiles, weight, cotangent)
    output, grad_input, grad_weight = pl.pallas_call(
        copy_kernel,
        out_shape=tuple(jax.ShapeDtypeStruct(x.shape, x.dtype) for x in results),
        in_specs=[vmem] * 3,
        out_specs=(vmem,) * 3,
        name="results",
    )(*results)
    return output, grad_weight, grad_input


def solution(mesh):
    placed = (
        P(("blk", "rep"), None),
        P("blk", "rep", None, None, None, None),
        P("blk", "rep", None, None),
        P("blk", "rep", None, None),
        P("blk", "rep", None),
        P(),
        P(("blk", "rep"), None),
    )
    return jax.shard_map(
        local,
        mesh=mesh,
        in_specs=placed,
        out_specs=(P(("blk", "rep"), None), P(), P(("blk", "rep"), None)),
        check_vma=False,
    )
```

```python
import functools
import math

import jax
import jax.numpy as jnp
from jax import lax
from jax.experimental import pallas as pl
from jax.experimental.pallas import tpu as pltpu
from jax.sharding import PartitionSpec as P

MESH = pl.DeviceIdType.MESH
F = 256
BS = 128
CAP = 12
PANELS = 32
PANEL = 512
HALF = 256
QUARTER = 128
SLOTS = PANELS * CAP
SENDS = 200
GW_AT = {1: 2, 2: 3, 3: 4, 6: 5, 7: 6, 9: 7}
bf16 = jnp.bfloat16
f32 = jnp.float32


class Place:
    def __init__(self):
        b = lax.axis_index("blk")
        r = lax.axis_index("rep")
        self.b, self.r = b, r
        self.c = {"x": lax.rem(b, 4), "z": lax.rem(b // 4, 4)}
        self.y = b // 16
        self.yp = 1 - self.y
        self.core = lax.rem(r, 2)
        self.yh = r // 2
        self.nb = {"y": {"blk": self.blk(self.yp, self.c["z"], self.c["x"])}}
        for axis in ("x", "z"):
            for name, step in (("+", 1), ("-", -1), ("2", 2)):
                self.nb[axis + name] = {"blk": self.at(self.y, axis, step, 0)}
        self.nb["core"] = {"rep": self.yh * 2 + 1 - self.core}
        self.nb["yh"] = {"rep": (1 - self.yh) * 2 + self.core}

    def blk(self, y, z, x):
        return y * 16 + z * 4 + x

    def up(self, axis, step):
        return lax.rem(self.c[axis] + step + 4, 4)

    def at(self, y, first, d, e):
        if first == "x":
            return self.blk(y, self.up("z", e), self.up("x", d))
        return self.blk(y, self.up("z", d), self.up("x", e))

    def on_second(self, y, first, d, e):
        if first == "x":
            return self.blk(y, e, self.up("x", d))
        return self.blk(y, self.up("z", d), e)

    def barrier(self, names):
        sem = pltpu.get_barrier_semaphore()
        for name in names:
            pl.semaphore_signal(sem, inc=1, device_id=self.nb[name], device_id_type=MESH)
        pl.semaphore_wait(sem, len(names))


class Sends:
    def __init__(self, place, send, recv):
        self.place, self.send, self.recv = place, send, recv
        self.count = 0
        self.pending = []

    def to(self, where, src, dst):
        t = self.count
        self.count += 1
        copy = pltpu.make_async_remote_copy(
            src, dst, self.send.at[t], self.recv.at[t],
            device_id=self.place.nb[where], device_id_type=MESH,
        )
        copy.start()
        self.pending.append(copy)
        return t

    def wait(self, t, dst):
        pltpu.make_async_remote_copy(
            dst, dst, self.send.at[t], self.recv.at[t],
            device_id=self.place.nb["y"], device_id_type=MESH,
        ).wait_recv()

    def drain(self):
        for copy in self.pending:
            copy.wait_send()


PARTS = (("x", "z", 0), ("z", "x", 1))


def load_tiles(tiles_hbm, tiles, sem):
    copies = [
        pltpu.make_async_copy(
            tiles_hbm.at[pl.ds(i * SLOTS // 4, SLOTS // 4)],
            tiles.at[pl.ds(i * SLOTS // 4, SLOTS // 4)],
            sem.at[i],
        )
        for i in range(4)
    ]
    for copy in copies:
        copy.start()
    return copies


def kernel(
    inv, f_ref, tiles_hbm, w_ref, ct_ref,
    out_ref, gi_ref, gw_ref,
    g, tiles, acc, in1, sbuf, in2, bt, gwp,
    pbuf, in_h, in_f, in_e, sb, in_h1, in_f1, tb, sy, in_y,
    gc, ga, gy, gq, gx, gz, gb, gr, go, send, recv, loc,
):
    me = Place()
    me.barrier(("x+", "x-", "x2", "z+", "z-", "z2", "y", "core", "yh"))
    sends = Sends(me, send, recv)
    y, yp = me.y, me.yp
    ys = (y, yp)

    def rows(blk, lo, n):
        return g.at[blk, pl.ds(lo, n)]

    def push(where, blk, lo, n, mine=False):
        src = f_ref.at[pl.ds(lo, n)] if mine else rows(blk, lo, n)
        return sends.to(where, src, rows(blk, lo, n))

    def arrive(t, blk, lo, n):
        sends.wait(t, rows(blk, lo, n))

    p1, p1f, p2, p2f, far2, far3 = {}, {}, {}, {}, {}, {}

    def start2(s, p, d, mine=False):
        blk = me.at(ys[s], p[0], d, 0)
        lo = p[2] * HALF
        down = push(p[1] + "-", blk, lo, HALF, mine)
        p2[s, p[2], d] = (push(p[1] + "+", blk, lo, HALF, mine) if s == 0 else None, down)

    def stage1(s, mine):
        for p in PARTS:
            blk = me.at(ys[s], p[0], 0, 0)
            lo = p[2] * HALF
            p1[s, p[2]] = (push(p[0] + "+", blk, lo, HALF, mine), push(p[0] + "-", blk, lo, HALF, mine))
        for p in PARTS:
            start2(s, p, 0, mine)

    def stage2(s):
        for p in PARTS:
            lo = p[2] * HALF
            t = p1[s, p[2]]
            at = functools.partial(me.at, ys[s], p[0])
            arrive(t[0], at(-1, 0), lo, HALF)
            f0 = push(p[0] + "+", at(-1, 0), lo, QUARTER)
            start2(s, p, -1)
            arrive(t[1], at(1, 0), lo, HALF)
            f1 = push(p[0] + "-", at(1, 0), lo + QUARTER, QUARTER)
            start2(s, p, 1)
            p1f[s, p[2]] = (f0, f1)

    def stage3(s):
        for p in PARTS:
            lo = p[2] * HALF
            f0, f1 = p1f[s, p[2]]
            arrive(f0, me.at(ys[s], p[0], 2, 0), lo, QUARTER)
            arrive(f1, me.at(ys[s], p[0], 2, 0), lo + QUARTER, QUARTER)
            start2(s, p, 2)

    def stage4(d):
        for p in PARTS:
            lo = p[2] * HALF
            t = p2[0, p[2], d]
            at = functools.partial(me.at, y, p[0])
            arrive(t[0], at(d, -1), lo, HALF)
            far2[p[2], d] = push("y", at(d, -1), lo, HALF)
            f0 = push(p[1] + "+", at(d, -1), lo, QUARTER)
            arrive(t[1], at(d, 1), lo, HALF)
            p2f[p[2], d] = (f0, push(p[1] + "-", at(d, 1), lo + QUARTER, QUARTER))

    def stage5(d):
        for p in PARTS:
            lo = p[2] * HALF
            blk = me.at(y, p[0], d, 2)
            arrive(p2f[p[2], d][0], blk, lo, QUARTER)
            arrive(p2f[p[2], d][1], blk, lo + QUARTER, QUARTER)

    def stage6(d):
        for p in PARTS:
            blk = me.at(yp, p[0], d, -1)
            arrive(far2[p[2], d], blk, p[2] * HALF, HALF)
            far3[p[2], d] = push(p[1] + "+", blk, p[2] * HALF, HALF)

    def stage7(d):
        for p in PARTS:
            arrive(p2[1, p[2], d][1], me.at(yp, p[0], d, 1), p[2] * HALF, HALF)

    def stage8(d):
        for p in PARTS:
            arrive(far3[p[2], d], me.at(yp, p[0], d, 2), p[2] * HALF, HALF)

    def product(half, s, panels):
        blks = [(me.at(ys[s], p[0], d, e), p[2]) for d, e in panels for p in PARTS]
        lhs = []
        for blk, k in blks:
            for v in range(2):
                base = half * 32 + k * 2 + v
                lhs.append(jnp.concatenate([tiles[inv[blk, base + h * 4]] for h in range(8)], axis=0))
        lhs = jnp.concatenate(lhs, axis=1)
        rhs = jnp.concatenate([g[blk, pl.ds(k * HALF, HALF), :] for blk, k in blks], axis=0)
        return jnp.dot(lhs, rhs, preferred_element_type=f32)

    def compute(s, *panels, first=False):
        @pl.loop(0, 2)
        def _(half):
            if first:
                acc[half] = product(half, s, panels)
            else:
                acc[half] += product(half, s, panels)

    far = 1 - me.yh
    other = 1 - me.core
    later = []

    def first_far(s, *panels):
        acc[far] += product(far, s, panels)
        later.append((s, panels))

    def catch_up(n):
        for s, panels in later[:n]:
            acc[me.yh] += product(me.yh, s, panels)
        del later[:n]

    stage1(0, True)
    to_y = [push("y", me.b, i * HALF, HALF, True) for i in range(2)]
    own = pltpu.make_async_copy(f_ref, g.at[me.b], loc.at[4])
    own.start()
    loads = load_tiles(tiles_hbm, tiles, loc)
    tiles[SLOTS] = jnp.zeros((BS, BS), bf16)
    stage2(0)
    own.wait()
    for copy in loads:
        copy.wait()
    compute(0, (0, 0), (-1, 0), first=True)
    stage4(0)
    twin = me.blk(yp, me.c["z"], me.c["x"])
    for i in range(2):
        arrive(to_y[i], twin, i * HALF, HALF)
    stage1(1, False)
    stage3(0)
    compute(0, (0, -1), (0, 1))
    compute(0, (1, 0), (2, 0))
    stage4(-1)
    compute(0, (-1, -1), (-1, 1))
    stage4(1)
    stage6(0)
    compute(0, (1, -1), (1, 1))
    stage2(1)
    stage5(0)
    compute(1, (0, 0), (-1, 0))
    stage6(-1)
    stage4(2)
    stage3(1)
    stage5(-1)
    compute(0, (2, -1), (2, 1))
    stage6(1)
    compute(0, (0, 2), (-1, 2))
    compute(1, (1, 0), (2, 0))
    stage5(1)
    stage6(2)
    stage5(2)
    first_far(0, (1, 2), (2, 2))
    first_far(1, (0, -1), (-1, -1))
    first_far(1, (1, -1), (2, -1))
    for d in (0, -1):
        stage7(d)
    first_far(1, (0, 1), (-1, 1))
    for d in (1, 2):
        stage7(d)
    first_far(1, (1, 1), (2, 1))
    for d in (0, -1):
        stage8(d)
    first_far(1, (0, 2), (-1, 2))
    for d in (1, 2):
        stage8(d)
    first_far(1, (1, 2), (2, 2))

    theirs = pl.ds(other * PANEL, PANEL)
    t_far = sends.to("core", acc.at[far, theirs], in1.at[far])
    catch_up(3)
    sends.wait(t_far, in1.at[far])
    t_yh = []
    for i in range(2):
        part = pl.ds(i * HALF, HALF)
        mine = acc[far, pl.ds(me.core * PANEL + i * HALF, HALF), :]
        sbuf[i] = (mine + in1[far, part, :]).astype(bf16)
        t_yh.append(sends.to("yh", sbuf.at[i], in2.at[i]))
    catch_up(len(later))
    t_near = sends.to("core", acc.at[me.yh, theirs], in1.at[me.yh])
    sends.wait(t_near, in1.at[me.yh])
    t_bt = []
    for i in range(2):
        part = pl.ds(i * HALF, HALF)
        sends.wait(t_yh[i], in2.at[i])
        mine = acc[me.yh, pl.ds(me.core * PANEL + i * HALF, HALF), :]
        agg = (mine + in1[me.yh, part, :] + in2[i].astype(f32)).astype(bf16)
        linear = jnp.dot(agg, w_ref[...], preferred_element_type=f32)
        sigma = 1.0 / (1.0 + jnp.exp(-linear))
        gl = (ct_ref[part, :].astype(f32) * sigma * (1.0 + linear * (1.0 - sigma))).astype(bf16)
        back = lax.dot_general(w_ref[...], gl, (((1,), (1,)), ((), ())), preferred_element_type=f32)
        mine = bt.at[me.r * 2 + i]
        bt[me.r * 2 + i] = back.astype(bf16)
        t_bt.append((sends.to("yh", mine, mine), sends.to("core", mine, mine)))
        out_ref[part, :] = (linear * sigma).astype(bf16)
        local_gw = lax.dot_general(agg, gl, (((0,), (0,)), ((), ())), preferred_element_type=f32)
        if i == 0:
            gwp[...] = local_gw
        else:
            gwp[...] += local_gw

    cx, cz = me.c["x"], me.c["z"]
    hops = ((1, "+"), (2, "2"), (3, "-"))
    gstate = {}

    def gw_step(n):
        t = gstate.get("t")
        if n == 0:
            gstate["t"] = sends.to("core", gwp.at[pl.ds(other * 128, 128)], gc)
        elif n == 1:
            sends.wait(t, gc)
            ga[...] = gwp[pl.ds(me.core * 128, 128), :] + gc[...]
            gstate["t"] = sends.to("y", ga.at[pl.ds(yp * 64, 64)], gy)
        elif n == 2:
            sends.wait(t, gy)
            gq[...] = ga[pl.ds(y * 64, 64), :] + gy[...]
            gstate["t"] = [
                sends.to("x" + name, gq.at[pl.ds(me.up("x", step) * 16, 16)], gx.at[i])
                for i, (step, name) in enumerate(hops)
            ]
        elif n == 3:
            total = gq[pl.ds(cx * 16, 16), :]
            for i in range(3):
                sends.wait(t[i], gx.at[i])
                total = total + gx[i]
            gz[cz] = total
            gstate["t"] = [sends.to("z" + name, gz.at[cz], gz.at[cz]) for _, name in hops]
        elif n == 4:
            for i, (step, _) in enumerate(hops):
                sends.wait(t[i], gz.at[me.up("z", -step)])
            gb[0] = (gz[0] + gz[1]) + (gz[2] + gz[3])
            gstate["t"] = sends.to("yh", gb.at[0], gb.at[1])
        elif n == 5:
            sends.wait(t, gb.at[1])
            gr[pl.ds(cx * 16, 16), :] = (gb[0] + gb[1]) * f32(1.0 / math.sqrt(65536))
            mine = gr.at[pl.ds(cx * 16, 16)]
            gstate["t"] = [sends.to("x" + name, mine, mine) for _, name in hops]
        elif n == 6:
            for i, (step, _) in enumerate(hops):
                sends.wait(t[i], gr.at[pl.ds(me.up("x", -step) * 16, 16)])
            go[pl.ds(y * 64, 64), :] = gr[...]
            mine = go.at[pl.ds(y * 64, 64)]
            gstate["t"] = sends.to("y", mine, mine)
        elif n == 7:
            sends.wait(t, go.at[pl.ds(yp * 64, 64)])
            gw_ref[pl.ds(me.core * 128, 128), :] = go[...]
            mine = gw_ref.at[pl.ds(me.core * 128, 128)]
            gstate["t"] = sends.to("core", mine, mine)
        elif n == 8:
            sends.wait(t, gw_ref.at[pl.ds(other * 128, 128)])

    gw_step(0)
    there = far * 2 + me.core
    b_fwd = []
    for i in range(2):
        src = bt.at[there * 2 + i]
        sends.wait(t_bt[i][0], src)
        b_fwd.append(sends.to("core", src, src))
    for i in range(2):
        sends.wait(t_bt[i][1], bt.at[(me.yh * 2 + other) * 2 + i])
        sends.wait(b_fwd[i], bt.at[(far * 2 + other) * 2 + i])

    D = (2, -1, 1, 0)
    lo, hi = pl.ds(0, QUARTER), pl.ds(QUARTER, QUARTER)
    halves, fulls, halves1, fulls1, to_e = {}, {}, {}, {}, {}

    def slot(s, d, p):
        return (s * 4 + D.index(d)) * 2 + p[2]

    def wide(ref, *at):
        return ref[at].astype(f32)

    def spread(s, d, p):
        q = slot(s, d, p)

        def pair(*es):
            cols = []
            for e in es:
                blk = me.at(ys[s], p[0], d, e)
                for v in range(2):
                    cols.append(jnp.concatenate([tiles[inv[blk, p[2] * 2 + v + h * 4]] for h in range(16)], axis=0))
            rhs = jnp.concatenate(cols, axis=1)
            lhs = jnp.concatenate([bt[i] for i in range(8)], axis=1)
            both = jnp.dot(lhs, rhs, preferred_element_type=f32).astype(bf16)
            for i, e in enumerate(es):
                pbuf[q, e] = both[:, i * HALF:(i + 1) * HALF]

        u = slot(0, d, p)
        if s == 1:
            pair(1, 3)
            fulls[q] = (
                sends.to(p[1] + "+", pbuf.at[q, 1], in_f.at[q, 0]),
                sends.to(p[1] + "-", pbuf.at[q, 3], in_f.at[q, 1]),
            )
            pair(2, 0)
            to_e[u] = sends.to("y", pbuf.at[q, 2], in_e.at[u])
        else:
            pair(2, 1)
            sends.wait(to_e[u], in_e.at[u])
            pbuf[q, 2] = (wide(pbuf, q, 2) + wide(in_e, u)).astype(bf16)
            halves[q] = (
                sends.to(p[1] + "+", pbuf.at[q, 2, lo], in_h.at[q, 0]),
                sends.to(p[1] + "-", pbuf.at[q, 2, hi], in_h.at[q, 1]),
            )
            pair(3, 0)

    def second(s, d, p):
        if s == 1:
            return
        q = slot(s, d, p)
        t = halves[q]
        sends.wait(t[0], in_h.at[q, 0])
        pbuf[q, 1, lo, :] = (pbuf[q, 1, lo, :].astype(f32) + wide(in_h, q, 0)).astype(bf16)
        up = sends.to(p[1] + "+", pbuf.at[q, 1], in_f.at[q, 0])
        sends.wait(t[1], in_h.at[q, 1])
        pbuf[q, 3, hi, :] = (pbuf[q, 3, hi, :].astype(f32) + wide(in_h, q, 1)).astype(bf16)
        down = sends.to(p[1] + "-", pbuf.at[q, 3], in_f.at[q, 1])
        fulls[q] = (up, down)

    def third(s, d, p):
        q = slot(s, d, p)
        t = fulls[q]
        u = s * 2 + p[2]
        sends.wait(t[0], in_f.at[q, 0])
        sends.wait(t[1], in_f.at[q, 1])
        total = wide(pbuf, q, 0) + wide(in_f, q, 0) + wide(in_f, q, 1)
        if d == 2:
            sb[u, 0] = total.astype(bf16)
            halves1[u] = (
                sends.to(p[0] + "+", sb.at[u, 0, lo], in_h1.at[u, 0]),
                sends.to(p[0] + "-", sb.at[u, 0, hi], in_h1.at[u, 1]),
            )
        elif d == 1:
            sb[u, 1] = total.astype(bf16)
            sends.wait(halves1[u][0], in_h1.at[u, 0])
            sb[u, 1, lo, :] = (total[:QUARTER] + wide(in_h1, u, 0)).astype(bf16)
            fulls1[u, 0] = sends.to(p[0] + "+", sb.at[u, 1], in_f1.at[u, 0])
        elif d == -1:
            sb[u, 2] = total.astype(bf16)
            sends.wait(halves1[u][1], in_h1.at[u, 1])
            sb[u, 2, hi, :] = (total[QUARTER:] + wide(in_h1, u, 1)).astype(bf16)
            fulls1[u, 1] = sends.to(p[0] + "-", sb.at[u, 2], in_f1.at[u, 1])
        else:
            tb[p[2]] = total

    home = {}

    def fourth(s, p):
        u = s * 2 + p[2]
        for i in range(2):
            sends.wait(fulls1[u, i], in_f1.at[u, i])
        total = tb[p[2]] + wide(in_f1, u, 0) + wide(in_f1, u, 1)
        if s == 1:
            sy[p[2]] = total.astype(bf16)
            home[p[2]] = sends.to("y", sy.at[p[2]], in_y.at[p[2]])
        else:
            sends.wait(home[p[2]], in_y.at[p[2]])
            total = total + wide(in_y, p[2])
            gi_ref[pl.ds(p[2] * HALF, HALF), :] = total.T

    steps = [(s, d) for s in (1, 0) for d in D]
    n = len(steps)

    def both(fn, step):
        for p in PARTS:
            fn(*step, p)

    gw_step(1)
    for i in range(n + 2):
        if i < n:
            both(spread, steps[i])
        if 1 <= i <= n:
            both(second, steps[i - 1])
        if i >= 2:
            both(third, steps[i - 2])
            if i - 2 == 3:
                for p in PARTS:
                    fourth(1, p)
        if i in GW_AT:
            gw_step(GW_AT[i])
    for p in PARTS:
        fourth(0, p)
    gw_step(8)
    sends.drain()
    assert sends.count <= SENDS


def copy_kernel(*refs):
    k = len(refs) // 2
    for i in range(k):
        refs[k + i][...] = refs[i][...]


def inverse(bands, cols, counts):
    slots = jnp.arange(CAP, dtype=jnp.int32)
    where = jnp.where(slots[None] < counts[:, None], bands * 4 + cols, -1)
    ids = jnp.arange(SLOTS, dtype=jnp.int32).reshape(PANELS, CAP) - SLOTS
    hit = where[:, None, :] == jnp.arange(64, dtype=jnp.int32)[None, :, None]
    return jnp.sum(jnp.where(hit, ids[:, None, :], 0), axis=2) + SLOTS


def local(features, tiles, bands, cols, counts, weight, cotangent):
    inv = inverse(bands[0, 0], cols[0, 0], counts[0, 0])
    tiles = tiles.reshape(SLOTS, BS, BS)
    vmem = pl.BlockSpec(memory_space=pltpu.VMEM)
    hbm = pl.BlockSpec(memory_space=pl.ANY)
    smem = pl.BlockSpec(memory_space=pltpu.SMEM)
    dma = pltpu.SemaphoreType.DMA
    results = (
        jax.ShapeDtypeStruct((PANEL, F), bf16),
        jax.ShapeDtypeStruct((PANEL, F), f32),
        jax.ShapeDtypeStruct((F, F), f32),
    )
    results = pl.pallas_call(
        kernel,
        out_shape=results,
        in_specs=[smem, vmem, hbm, vmem, vmem],
        out_specs=(vmem, vmem, vmem),
        scratch_shapes=[
            pltpu.VMEM((PANELS, PANEL, F), bf16),
            pltpu.VMEM((SLOTS + 1, BS, BS), bf16),
            pltpu.VMEM((2, 2 * PANEL, F), f32),
            pltpu.VMEM((2, PANEL, F), f32),
            pltpu.VMEM((2, HALF, F), bf16),
            pltpu.VMEM((2, HALF, F), bf16),
            pltpu.VMEM((8, F, HALF), bf16),
            pltpu.VMEM((F, F), f32),
            pltpu.VMEM((16, 4, F, HALF), bf16),
            pltpu.VMEM((8, 2, QUARTER, HALF), bf16),
            pltpu.VMEM((16, 2, F, HALF), bf16),
            pltpu.VMEM((8, F, HALF), bf16),
            pltpu.VMEM((4, 3, F, HALF), bf16),
            pltpu.VMEM((4, 2, QUARTER, HALF), bf16),
            pltpu.VMEM((4, 2, F, HALF), bf16),
            pltpu.VMEM((2, F, HALF), f32),
            pltpu.VMEM((2, F, HALF), bf16),
            pltpu.VMEM((2, F, HALF), bf16),
            pltpu.VMEM((128, F), f32),
            pltpu.VMEM((128, F), f32),
            pltpu.VMEM((64, F), f32),
            pltpu.VMEM((64, F), f32),
            pltpu.VMEM((3, 16, F), f32),
            pltpu.VMEM((4, 16, F), f32),
            pltpu.VMEM((2, 16, F), f32),
            pltpu.VMEM((64, F), f32),
            pltpu.VMEM((128, F), f32),
            dma((SENDS,)), dma((SENDS,)), dma((5,)),
        ],
        compiler_params=pltpu.CompilerParams(
            collective_id=0, has_side_effects=True, vmem_limit_bytes=58 * 2**20
        ),
        name="graph_layer",
    )(inv, features, tiles, weight, cotangent)
    output, grad_input, grad_weight = pl.pallas_call(
        copy_kernel,
        out_shape=tuple(jax.ShapeDtypeStruct(x.shape, x.dtype) for x in results),
        in_specs=[vmem] * 3,
        out_specs=(vmem,) * 3,
        name="results",
    )(*results)
    return output, grad_weight, grad_input


def solution(mesh):
    placed = (
        P(("blk", "rep"), None),
        P("blk", "rep", None, None, None, None),
        P("blk", "rep", None, None),
        P("blk", "rep", None, None),
        P("blk", "rep", None),
        P(),
        P(("blk", "rep"), None),
    )
    return jax.shard_map(
        local,
        mesh=mesh,
        in_specs=placed,
        out_specs=(P(("blk", "rep"), None), P(), P(("blk", "rep"), None)),
        check_vma=False,
    )
```
